32 devices in a mesh: lat: 8 (over z, y), lon: 4 (over x, core).
Axes of the slice: x: 2, y: 2, z: 4, core: 2. Of those that a mesh axis runs over, the one named last changes fastest.
Arguments:
- tokens: bfloat16 [2, 96, 192, 512], P(None, 'lat', 'lon'), may hold values from -12 to 12
- gains: float32 [4, 512], replicated, may hold values from 0.1 to 1.9
- w_qkv: bfloat16 [2, 512, 1536], replicated, may hold values from -10 to 10
- w_proj: bfloat16 [2, 512, 512], replicated, may hold values from -0.25 to 0.25
- w_in: bfloat16 [2, 512, 1024], replicated, may hold values from -0.25 to 0.25
- w_out: bfloat16 [2, 1024, 512], replicated, may hold values from -0.1875 to 0.1875
Outputs:
- evolved: bfloat16 [2, 96, 192, 512], P(None, 'lat', 'lon')
The draws below stay inside these ranges and needn't reach their ends.
All inputs are finite; a program needn't handle non-finite values.
Results may differ from the reference program's by a relative error of at most 0.013.
The reference program's roundings to bfloat16 on the way count: a program that leaves them out, or rounds other values in their place, can miss the bound.
Values may be sent and summed in bfloat16 or wider, within the bound.
No kernel may reach another device: no remote copies, remote signals or barrier semaphores. Data moves between devices by JAX's collectives and lax.ppermute only.
A program may use at most 128 MiB of HBM per device.

```python
import math
import jax
import jax.numpy as jnp
from jax import lax

D = 512
HEADS = 16
FF = 1024
LEV = 2
WZ = 2
WY = 12
WX = 6
SZ = 1
SY = 6
SX = 3
NLAT = 96
NLON = 192


def draw_tokens(key, part):
    key = jax.random.fold_in(key, 11)
    row_key = jax.random.fold_in(key, 0)
    col_key = jax.random.fold_in(key, 1)
    noise_key = jax.random.fold_in(key, 3)
    grid_shape = (LEV, NLAT, NLON, D)
    col_scale = jnp.exp(jax.random.uniform(col_key, (D,), jnp.float32, math.log(0.3), math.log(3.0)))
    row_scale = jnp.exp(jax.random.uniform(row_key, (LEV, NLAT, NLON, 1), jnp.float32, math.log(0.4), math.log(4.0)))
    values = row_scale * col_scale * jax.random.normal(noise_key, grid_shape, jnp.float32)
    return jnp.clip(values, -12.0, 12.0).astype(jnp.bfloat16)


def draw_w_qkv(key, part):
    key = jax.random.fold_in(key, 12)
    base_key = jax.random.fold_in(key, 0)
    limit = 4.0 * D ** (-0.5)
    base = jnp.clip(jax.random.normal(base_key, (2, D, 3 * D), jnp.float32) * D ** (-0.5), -limit, limit)
    return base.astype(jnp.bfloat16)


def normal_values(rng, extent, deviation, most, kind=jnp.bfloat16):
    values = jax.random.normal(rng, extent, jnp.float32) * deviation
    return jnp.minimum(jnp.maximum(values, -most), most).astype(kind)


def setup_inputs(seed: int = 0) -> dict:
    keys = jax.random.split(jax.random.key(seed), 7)
    tokens = draw_tokens(jax.random.fold_in(keys[6], 71), 0)
    gains = jnp.clip(1.0 + 0.18 * jax.random.normal(keys[1], (4, D), jnp.float32), 0.1, 1.9)
    w_qkv = draw_w_qkv(jax.random.fold_in(keys[6], 71), 0)
    w_proj = normal_values(keys[3], (2, D, D), D ** -0.5, 0.25)
    w_in = normal_values(keys[4], (2, D, FF), D ** -0.5, 0.25)
    w_out = normal_values(keys[5], (2, FF, D), FF ** -0.5, 0.1875)
    return dict(tokens=tokens, gains=gains, w_qkv=w_qkv, w_proj=w_proj, w_in=w_in, w_out=w_out)


EPSILON = 1e-05
NEGATIVE = -1e+30

def layer_norm(values, gain_row):
    widened = values.astype(jnp.float32)
    centered = widened - lax.optimization_barrier(jnp.mean(widened, axis=-1, keepdims=True))
    variance = lax.optimization_barrier(jnp.mean(centered * centered, axis=-1, keepdims=True))
    return (centered * lax.rsqrt(variance + EPSILON) * gain_row).astype(jnp.bfloat16)

def to_windows(grid, win_depth, win_rows, win_cols):
    levels, height, breadth, channels = grid.shape
    parted = grid.reshape(levels // win_depth, win_depth, height // win_rows, win_rows, breadth // win_cols, win_cols, channels)
    parted = parted.transpose(0, 2, 4, 1, 3, 5, 6)
    return parted.reshape(-1, win_depth * win_rows * win_cols, channels)

def from_windows(parted, grid_shape, win_depth, win_rows, win_cols):
    levels, height, breadth, channels = grid_shape
    grid = parted.reshape(levels // win_depth, height // win_rows, breadth // win_cols, win_depth, win_rows, win_cols, channels)
    grid = grid.transpose(0, 3, 1, 4, 2, 5, 6)
    return grid.reshape(levels, height, breadth, channels)

def attend(queries, keys_part, values_part, allowed):
    windows, members, channels = queries.shape
    head_size = channels // HEADS
    split_shape = (windows, members, HEADS, head_size)
    scores = jnp.einsum('wqhe,wkhe->whqk', queries.reshape(split_shape).astype(jnp.float32), keys_part.reshape(split_shape).astype(jnp.float32)) * head_size ** (-0.5)
    if allowed is not None:
        scores = jnp.where(allowed[:, None], scores, NEGATIVE)
    largest = lax.optimization_barrier(jnp.max(scores, axis=-1, keepdims=True))
    powers = jnp.exp(scores - largest)
    weights = (powers / lax.optimization_barrier(jnp.sum(powers, axis=-1, keepdims=True))).astype(jnp.bfloat16)
    mixed = jnp.einsum('whqk,wkhe->wqhe', weights.astype(jnp.float32), values_part.reshape(split_shape).astype(jnp.float32))
    return mixed.reshape(windows, members, channels).astype(jnp.bfloat16)

def finish(tokens, attended, gains, layer_id, w_proj, w_in, w_out):
    mixed = (tokens.astype(jnp.float32) + jnp.dot(attended, w_proj[layer_id], preferred_element_type=jnp.float32)).astype(jnp.bfloat16)
    normed = layer_norm(mixed, gains[2 * layer_id + 1])
    hidden = jax.nn.gelu(jnp.dot(normed, w_in[layer_id], preferred_element_type=jnp.float32), approximate=True).astype(jnp.bfloat16)
    return (mixed.astype(jnp.float32) + jnp.dot(hidden, w_out[layer_id], preferred_element_type=jnp.float32)).astype(jnp.bfloat16)

def run_block(tokens, gains, layer_id, w_qkv, w_proj, w_in, w_out, shifted):
    if shifted:
        tokens = jnp.roll(tokens, (-SZ, -SY, -SX), axis=(0, 1, 2))
    levels, height, breadth, channels = tokens.shape
    band_count = height // WY
    bands = tokens.reshape(levels, band_count, WY, breadth, channels).transpose(1, 0, 2, 3, 4)
    members = WZ * WY * WX
    level_of = (jnp.arange(members) // (WY * WX)).astype(jnp.int32)
    lower_side = (jnp.arange(members) // WX % WY >= SY).astype(jnp.int32)

    def one_band(carried):
        band, number = carried
        normed = layer_norm(band, gains[2 * layer_id])
        packed = jnp.dot(normed, w_qkv[layer_id], preferred_element_type=jnp.float32).astype(jnp.bfloat16)
        parted = to_windows(packed, WZ, WY, WX)
        allowed = None
        if shifted:
            group = level_of * 2 + jnp.where(number == band_count - 1, lower_side, jnp.zeros_like(lower_side))
            allowed = (group[:, None] == group[None, :])[None]
        result = attend(parted[..., :channels], parted[..., channels:2 * channels], parted[..., 2 * channels:], allowed)
        attended = from_windows(result, band.shape, WZ, WY, WX)
        return finish(band, attended, gains, layer_id, w_proj, w_in, w_out)
    done = lax.map(one_band, (bands, jnp.arange(band_count, dtype=jnp.int32)))
    done = done.transpose(1, 0, 2, 3, 4).reshape(levels, height, breadth, channels)
    if shifted:
        done = jnp.roll(done, (SZ, SY, SX), axis=(0, 1, 2))
    return done

def reference(tokens, gains, w_qkv, w_proj, w_in, w_out):
    first = run_block(tokens, gains, 0, w_qkv, w_proj, w_in, w_out, False)
    return run_block(first, gains, 1, w_qkv, w_proj, w_in, w_out, True)
```

```python
import jax
import jax.numpy as jnp
import numpy as np
from jax import lax
from jax.experimental import pallas as pl
from jax.experimental.pallas import tpu as pltpu
from jax.sharding import PartitionSpec as P

HEADS = 16
WY = 12
WX = 6
SY = 6
SX = 3
EPSILON = 1e-05
NEGATIVE = -1e30
BF = jnp.bfloat16
F32 = jnp.float32
GROUP = 4
EXP_SCALE = float(32.0 ** -0.5 * np.log2(np.e))


def norm(values, gain_row):
    centered = values - jnp.mean(values, axis=-1, keepdims=True)
    variance = jnp.mean(centered * centered, axis=-1, keepdims=True)
    return (centered * lax.rsqrt(variance + EPSILON) * gain_row).astype(BF)


def dot(a, b):
    return jnp.dot(a, b, preferred_element_type=F32)


def attend(q, k, v, bias):
    n, channels = q.shape
    head = channels // HEADS
    lane = lax.broadcasted_iota(jnp.int32, (1, 128), 1) // head
    lanes = lax.broadcasted_iota(jnp.int32, (n, 128), 1) // head
    pieces = []
    for g in range(channels // 128):
        cut = slice(128 * g, 128 * g + 128)
        qg = q[:, cut]
        stacked = jnp.concatenate(
            [qg * (lane == j).astype(F32) for j in range(GROUP)], axis=0
        ).astype(BF)
        s = lax.dot_general(
            stacked, k[:, cut], (((1,), (1,)), ((), ())), preferred_element_type=F32
        )
        if bias is not None:
            s = s + jnp.concatenate([bias] * GROUP, axis=0)
        p = jnp.exp2((s - jnp.max(s, axis=-1, keepdims=True)) * EXP_SCALE)
        w = (p * (1.0 / jnp.sum(p, axis=-1, keepdims=True))).astype(BF)
        o = dot(w, v[:, cut])
        total = o[:n]
        for j in range(1, GROUP):
            total = jnp.where(lanes == j, o[j * n : (j + 1) * n], total)
        pieces.append(total)
    return jnp.concatenate(pieces, axis=1)


def finish(x, attended, gain_row, w_proj, w_in, w_out):
    mixed = (x.astype(F32) + dot(attended, w_proj)).astype(BF)
    normed = norm(mixed.astype(F32), gain_row)
    h = dot(normed, w_in)
    h = jax.nn.gelu(h, approximate=True).astype(BF)
    return mixed.astype(F32) + dot(h, w_out)


def block0(x_ref, perm_ref, gains_ref, wqkv_ref, wproj_ref, win_ref, wout_ref,
           x1_ref, n1_ref, xs, qkv, att, xf):
    tokens, channels = xs.shape
    half = tokens // 2
    strips = half // 72
    quarter = half // 2
    perm = perm_ref[...]
    parts = []
    for r in range(2):
        nat = jnp.concatenate([x_ref[z, quarter * r : quarter * (r + 1)] for z in range(2)], axis=0)
        parts.append(dot(perm, nat).reshape(strips, 72, channels))
    x = jnp.concatenate(parts, axis=1).reshape(tokens, channels)
    xs[...] = x.astype(BF)
    rows = 2 * 144
    steps = tokens // rows

    def project(i, _):
        at = pl.ds(pl.multiple_of(i * rows, 16), rows)
        normed = norm(xs[at].astype(F32), gains_ref[0:1])
        qkv[at] = dot(normed, wqkv_ref[0]).astype(BF)
        return 0

    lax.fori_loop(0, steps, project, 0)

    def window(i, _):
        at = pl.ds(pl.multiple_of(i * 144, 16), 144)
        q = qkv[at, :channels].astype(F32)
        att[at] = attend(q, qkv[at, channels : 2 * channels], qkv[at, 2 * channels :], None).astype(BF)
        return 0

    lax.fori_loop(0, strips, window, 0)

    def close(i, _):
        at = pl.ds(pl.multiple_of(i * rows, 16), rows)
        xf[at] = finish(xs[at], att[at], gains_ref[1:2], wproj_ref[0], win_ref[0], wout_ref[0])
        return 0

    lax.fori_loop(0, steps, close, 0)
    for r in range(2):
        mine = xf[...].reshape(strips, 2, 72, channels)[:, r].reshape(half, channels)
        mine = pltpu.roll(mine, 36, 0).astype(BF)
        x1_ref[r] = mine
        n1_ref[r] = norm(mine.astype(F32), gains_ref[2:3])


def block1(x_ref, n_ref, top_ref, bot_ref, left_ref, right_ref, tl_ref, tr_ref, bl_ref, br_ref,
           bias_ref, perm_ref, gains_ref, wqkv_ref, wproj_ref, win_ref, wout_ref,
           out_ref, lhs, qs, kv, os, done):
    _, half, channels = x_ref.shape
    strips = half // 72
    wins = strips + 1
    first = lax.broadcasted_iota(jnp.int32, (72, channels), 0) < 36
    quarter = half // 2
    sides = (
        (top_ref, tl_ref, tr_ref),
        (bot_ref, bl_ref, br_ref),
    )

    def extend(own, left, right):
        own = own.astype(F32).reshape(strips, 72, channels)
        lead = jnp.where(first, left.astype(F32), own[0])
        tail = jnp.where(first, own[0], right.astype(F32))
        return jnp.concatenate([lead[None], own[1:], tail[None]], axis=0)

    for r in range(2):
        own = extend(n_ref[r], left_ref[r], right_ref[r])
        far_ref, fl_ref, fr_ref = sides[r]
        far = extend(far_ref[...], fl_ref[...], fr_ref[...])
        both = jnp.concatenate([own, far], axis=1).reshape(wins * 144, channels)
        lhs[...] = both.astype(BF)
        q = dot(own.reshape(wins * 72, channels).astype(BF), wqkv_ref[0, :, :channels])
        qs[...] = q.astype(BF).astype(F32).reshape(wins, 72, channels)
        rows = 3 * 144

        def project(i, _):
            at = pl.ds(pl.multiple_of(i * rows, 16), rows)
            kv[at] = dot(lhs[at], wqkv_ref[0, :, channels:]).astype(BF)
            return 0

        lax.fori_loop(0, wins * 144 // rows, project, 0)

        def window(i, _):
            at = pl.ds(pl.multiple_of(i * 144, 16), 144)
            os[i] = attend(qs[i], kv[at, :channels], kv[at, channels:], bias_ref[r])
            return 0

        lax.fori_loop(0, wins, window, 0)
        edge = jnp.where(first, os[wins - 1], os[0])
        attended = jnp.concatenate([edge[None], os[1:strips]], axis=0).reshape(half, channels).astype(BF)
        for i in range(2):
            at = slice(i * quarter, (i + 1) * quarter)
            done[at] = finish(
                x_ref[r, at], attended[at], gains_ref[3:4], wproj_ref[0], win_ref[0], wout_ref[0]
            ).astype(BF)
        nat = dot(perm_ref[...], done[...]).astype(BF)
        for z in range(2):
            out_ref[z, quarter * r : quarter * (r + 1)] = nat[quarter * z : quarter * (z + 1)]


def orders(strips):
    unit, lev, row, col = np.meshgrid(
        np.arange(2 * strips), np.arange(2), np.arange(SY), np.arange(SX), indexing="ij"
    )
    breadth = WX * strips
    return (lev * SY * breadth + row * breadth + unit * SX + col).reshape(-1)


def whole(shape):
    return pl.BlockSpec(shape, lambda i, n=len(shape): (0,) * n)


def layer(shape, index):
    return pl.BlockSpec((1,) + shape[1:], lambda i: (index, 0, 0))


def shards(tokens, gains, w_qkv, w_proj, w_in, w_out):
    levels, height, breadth, channels = tokens.shape
    half = levels * SY * breadth
    strips = breadth // WX
    order = orders(strips)
    onehot = np.zeros((half, half), np.float32)
    onehot[np.arange(half), order] = 1.0
    back = np.roll(onehot, 36, axis=0).T
    params = pltpu.CompilerParams(
        dimension_semantics=("arbitrary",), vmem_limit_bytes=56 * 1024 * 1024
    )
    weights = (w_qkv, w_proj, w_in, w_out)
    tile = (2, half, channels)
    x1, n1 = pl.pallas_call(
        block0,
        grid=(1,),
        in_specs=[whole((2, half, channels)), whole((half, half)), whole(gains.shape)]
        + [layer(w.shape, 0) for w in weights],
        out_specs=[whole(tile), whole(tile)],
        out_shape=[jax.ShapeDtypeStruct(tile, BF)] * 2,
        scratch_shapes=[
            pltpu.VMEM((2 * half, channels), BF),
            pltpu.VMEM((2 * half, 3 * channels), BF),
            pltpu.VMEM((2 * half, channels), BF),
            pltpu.VMEM((2 * half, channels), F32),
        ],
        compiler_params=params,
        name="regular",
    )(tokens.reshape(2, half, channels), jnp.asarray(onehot, BF), gains, *weights)

    lats, lons = lax.axis_size("lat"), lax.axis_size("lon")

    def move(block, dlat, dlon):
        route = [
            ((y + dlat) * lons + (x + dlon) % lons, y * lons + x)
            for y in range(lats)
            for x in range(lons)
            if 0 <= y + dlat < lats
        ]
        return lax.ppermute(block, ("lat", "lon"), route)

    bot = move(n1[0], 1, 0)
    top = move(n1[1], -1, 0)
    edge = n1[:, :72]
    left, right = move(edge, 0, -1), move(edge, 0, 1)
    tl, tr = move(edge[1], -1, -1), move(edge[1], -1, 1)
    bl, br = move(edge[0], 1, -1), move(edge[0], 1, 1)

    place = lax.axis_index("lat")
    token = np.arange(72)
    lev = token % 36 // 18
    same = np.tile(lev[:, None] == lev[None, :], (1, 2))
    far = np.arange(144) >= 72
    dead = jnp.stack([place == 0, place == lats - 1])
    allowed = same[None] & ~(dead[:, None, None] & far[None, None, :])
    bias = jnp.where(allowed, 0.0, NEGATIVE).astype(F32)
    wins = strips + 1
    out = pl.pallas_call(
        block1,
        grid=(1,),
        in_specs=[whole(a.shape) for a in (x1, n1, top, bot, left, right, tl, tr, bl, br, bias)]
        + [whole((half, half)), whole(gains.shape)]
        + [layer(w.shape, 1) for w in weights],
        out_specs=whole(tile),
        out_shape=jax.ShapeDtypeStruct(tile, BF),
        scratch_shapes=[
            pltpu.VMEM((wins * 144, channels), BF),
            pltpu.VMEM((wins, 72, channels), F32),
            pltpu.VMEM((wins * 144, 2 * channels), BF),
            pltpu.VMEM((wins, 72, channels), F32),
            pltpu.VMEM((half, channels), BF),
        ],
        compiler_params=params,
        name="shifted",
    )(x1, n1, top, bot, left, right, tl, tr, bl, br, bias, jnp.asarray(back, BF), gains, *weights)
    return out.reshape(tokens.shape)


def solution(mesh):
    in_specs = (P(None, "lat", "lon", None), P(), P(), P(), P(), P())
    out_specs = P(None, "lat", "lon", None)
    return jax.shard_map(shards, mesh=mesh, in_specs=in_specs, out_specs=out_specs, check_vma=False)
```

```python
import functools

import jax
import jax.numpy as jnp
import numpy as np
from jax import lax
from jax.experimental import pallas as pl
from jax.experimental.pallas import tpu as pltpu
from jax.sharding import PartitionSpec as P

HEADS = 16
WY = 12
WX = 6
SY = 6
SX = 3
EPSILON = 1e-05
NEGATIVE = -1e30
BF = jnp.bfloat16
F32 = jnp.float32
UNIT = 36
WIDTH0 = 128
WIDTH1 = 256
EXP_SCALE = float(32.0 ** -0.5 * np.log2(np.e))


def norm(values, gain_row):
    centered = values - jnp.mean(values, axis=-1, keepdims=True)
    variance = jnp.mean(centered * centered, axis=-1, keepdims=True)
    return (centered * lax.rsqrt(variance + EPSILON) * gain_row).astype(BF)


def dot(a, b):
    return jnp.dot(a, b, preferred_element_type=F32)


def attend(q, k, v, bias, width):
    n, channels = q.shape
    head = channels // HEADS
    count = width // head
    lane = lax.broadcasted_iota(jnp.int32, (1, width), 1) // head
    lanes = lax.broadcasted_iota(jnp.int32, (n, width), 1) // head
    pieces = []
    for g in range(channels // width):
        cut = slice(width * g, width * (g + 1))
        qg = q[:, cut]
        stacked = jnp.concatenate(
            [qg * (lane == j).astype(F32) for j in range(count)], axis=0
        ).astype(BF)
        s = lax.dot_general(
            stacked, k[:, cut], (((1,), (1,)), ((), ())), preferred_element_type=F32
        )
        if bias is not None:
            s = s + jnp.concatenate([bias] * count, axis=0)
        p = jnp.exp2((s - jnp.max(s, axis=-1, keepdims=True)) * EXP_SCALE).astype(BF)
        vg = v[:, cut]
        o = dot(p, jnp.concatenate([vg, jnp.ones((vg.shape[0], 128), BF)], axis=1))
        scale = 1.0 / o[:, width:]
        if width > 128:
            scale = jnp.concatenate([scale] * (width // 128), axis=1)
        o = o[:, :width] * scale
        total = o[:n]
        for j in range(1, count):
            total = jnp.where(lanes == j, o[j * n : (j + 1) * n], total)
        pieces.append(total)
    return jnp.concatenate(pieces, axis=1)


def finish(x, attended, gain_row, w_proj, w_in, w_out):
    mixed = (x.astype(F32) + dot(attended, w_proj)).astype(BF)
    normed = norm(mixed.astype(F32), gain_row)
    h = dot(normed, w_in)
    h = jax.nn.gelu(h, approximate=True).astype(BF)
    return mixed.astype(F32) + dot(h, w_out)


def block0(keep, side_ref, x_ref, *refs):
    *halos, perm_ref, gains_ref, wqkv_ref, wproj_ref, win_ref, wout_ref = refs[:-7]
    x1_ref, cross_ref, same_ref, xs, qkv, att, xf = refs[-7:]
    tokens, channels = xs.shape
    half = tokens // 2
    strips = half // 72
    quarter = x_ref.shape[1] // 2
    perm = perm_ref[...]
    parts = []
    for r in range(2):
        nat = [x_ref[z, quarter * r : quarter * (r + 1)] for z in range(2)]
        if halos:
            nat.append(
                jnp.concatenate([h[r].astype(F32) for h in halos], axis=0).astype(BF)
            )
        nat = jnp.concatenate(nat, axis=0)
        parts.append(dot(perm, nat).reshape(strips, 72, channels))
    x = jnp.concatenate(parts, axis=1).reshape(tokens, channels)
    xs[...] = x.astype(BF)
    qkv[...] = dot(norm(x, gains_ref[0:1]), wqkv_ref[0]).astype(BF)

    def window(i, _):
        at = pl.ds(pl.multiple_of(i * 144, 16), 144)
        q = qkv[at, :channels].astype(F32)
        k, v = qkv[at, channels : 2 * channels], qkv[at, 2 * channels :]
        att[at] = attend(q, k, v, None, WIDTH0).astype(BF)
        return 0

    lax.fori_loop(0, strips, window, 0)
    new = finish(xs[...], att[...], gains_ref[1:2], wproj_ref[0], win_ref[0], wout_ref[0])
    new = new.reshape(strips, 2, 72, channels)
    for r in range(2):
        xf[r] = new[:, r].reshape(half, channels)
    odd = side_ref[0]
    for g, n_ref in ((0, cross_ref), (1, same_ref)):
        mine = pltpu.roll(xf[jnp.where(odd == 0, g, 1 - g)], UNIT, 0).astype(BF)
        x1_ref[g] = mine[:keep]
        n_ref[...] = norm(mine.astype(F32), gains_ref[2:3])[:keep]


def blocks(rows):
    return rows.astype(F32).reshape(-1, 72, rows.shape[-1])


def windows(own, far, bias_ref, wqkv_ref, lhs, qs, kv, os):
    count, _, channels = own.shape
    lhs[...] = jnp.concatenate([own, far], axis=1).reshape(count * 144, channels).astype(BF)
    q = dot(own.reshape(count * 72, channels).astype(BF), wqkv_ref[0, :, :channels])
    qs[...] = q.astype(BF).astype(F32).reshape(count, 72, channels)
    rows = count * 72

    def project(i, _):
        at = pl.ds(pl.multiple_of(i * rows, 16), rows)
        kv[at] = dot(lhs[at], wqkv_ref[0, :, channels:]).astype(BF)
        return 0

    lax.fori_loop(0, 2, project, 0)

    def window(i, _):
        at = pl.ds(pl.multiple_of(i * 144, 16), 144)
        bias = bias_ref[i // (count // 2)]
        os[i] = attend(qs[i], kv[at, :channels], kv[at, channels:], bias, WIDTH1)
        return 0

    lax.fori_loop(0, count, window, 0)


def early(x_ref, cross_ref, same_ref, far_cross_ref, far_same_ref, bias_ref,
          gains_ref, wqkv_ref, wproj_ref, win_ref, wout_ref, out_ref, lhs, qs, kv, os):
    channels = x_ref.shape[-1]

    def pair(a_ref, b_ref):
        return jnp.concatenate([blocks(a_ref[...])[1:], blocks(b_ref[...])[1:]], axis=0)

    own, far = pair(cross_ref, same_ref), pair(far_cross_ref, far_same_ref)
    windows(own, far, bias_ref, wqkv_ref, lhs, qs, kv, os)
    rows = own.shape[0] * 72
    x = jnp.concatenate([blocks(x_ref[g])[1:] for g in range(2)], axis=0).reshape(rows, channels)
    attended = os[...].reshape(rows, channels).astype(BF)
    out_ref[...] = finish(
        x, attended, gains_ref[3:4], wproj_ref[0], win_ref[0], wout_ref[0]
    ).astype(BF)


def late(side_ref, done_ref, xa_ref, xb_ref, ca_ref, sa_ref, cb_ref, sb_ref,
         fca_ref, fsa_ref, fcb_ref, fsb_ref, bias_ref,
         perm_ref, gains_ref, wqkv_ref, wproj_ref, win_ref, wout_ref,
         out_ref, lhs, qs, kv, os, tile_ref):
    channels = xa_ref.shape[-1]
    first = lax.broadcasted_iota(jnp.int32, (72, channels), 0) < UNIT

    def extend(a, b):
        a, b = blocks(a), blocks(b)
        mid, lead = jnp.where(first, a[0], b[0]), jnp.where(first, b[0], a[0])
        return jnp.concatenate([mid[None], b[1:], lead[None]], axis=0)

    own = jnp.concatenate(
        [extend(ca_ref[...], cb_ref[...]), extend(sa_ref[...], sb_ref[...])], axis=0
    )
    far = jnp.concatenate(
        [extend(fca_ref[...], fcb_ref[...]), extend(fsa_ref[...], fsb_ref[...])], axis=0
    )
    windows(own, far, bias_ref, wqkv_ref, lhs, qs, kv, os)
    count = own.shape[0] // 2
    last = count - 2
    xs, atts = [], []
    for g in range(2):
        a, b = blocks(xa_ref[g]), blocks(xb_ref[g])
        o = os[count * g : count * (g + 1)]
        xs += [
            jnp.where(first, b[last], a[0])[None],
            jnp.where(first, a[0], b[0])[None],
            b[1:last],
        ]
        atts += [jnp.where(first, o[last], o[count - 1])[None], o[:last]]
    rows = (count - 1) * 72
    x = jnp.concatenate(xs, axis=0).reshape(2 * rows, channels)
    attended = jnp.concatenate(atts, axis=0).reshape(2 * rows, channels).astype(BF)
    new = finish(x, attended, gains_ref[3:4], wproj_ref[0], win_ref[0], wout_ref[0])
    ready = done_ref[...].astype(F32)
    share = ready.shape[0] // 2
    odd = side_ref[0]
    for g in range(2):
        tile_ref[:72] = new[rows * g : rows * g + 72]
        tile_ref[72 : 72 + share] = ready[share * g : share * (g + 1)]
        tile_ref[72 + share :] = new[rows * g + 72 : rows * (g + 1)]
        nat = dot(perm_ref[...], tile_ref[...].astype(BF)).astype(BF)
        quarter = nat.shape[0] // 2
        r = jnp.where(odd == 0, g, 1 - g)
        for z in range(2):
            out_ref[z, r] = nat[quarter * z : quarter * (z + 1)]


def orders(strips):
    unit, lev, row, col = np.meshgrid(
        np.arange(2 * strips), np.arange(2), np.arange(SY), np.arange(SX), indexing="ij"
    )
    breadth = WX * strips
    return (lev * SY * breadth + row * breadth + unit * SX + col).reshape(-1)


def whole(shape):
    return pl.BlockSpec(shape, lambda i, n=len(shape): (0,) * n)


def layer(shape, index):
    return pl.BlockSpec((1,) + shape[1:], lambda i: (index, 0, 0))


def tables(breadth):
    strips = breadth // WX
    order = orders(strips)
    half = order.size
    onehot = np.zeros((half, half), np.float32)
    onehot[np.arange(half), order] = 1.0
    cut = 72 * (strips // 2 + 1)
    halo = np.zeros((72, 72), np.float32)
    halo[np.arange(72), orders(1)] = 1.0
    rest = np.zeros((half - cut + 144, half + 144), np.float32)
    rest[: half - cut, :half] = onehot[cut:]
    rest[half - cut : half - cut + 72, half : half + 72] = halo
    rest[half - cut + 72 :, half + 72 :] = halo
    made = (onehot[:cut], rest, np.roll(onehot, UNIT, axis=0).T)
    return tuple(jnp.asarray(m, BF) for m in made)


PARAMS = pltpu.CompilerParams(
    dimension_semantics=("arbitrary",), vmem_limit_bytes=56 * 1024 * 1024
)


def call(body, name, scalars, arrays, extra, weights, index, outs, scratch):
    return pl.pallas_call(
        body,
        grid=(1,),
        in_specs=[pl.BlockSpec(memory_space=pltpu.SMEM) for _ in scalars]
        + [whole(a.shape) for a in arrays + extra]
        + [layer(w.shape, index) for w in weights],
        out_specs=[whole(o) for o in outs],
        out_shape=[jax.ShapeDtypeStruct(o, BF) for o in outs],
        scratch_shapes=scratch,
        compiler_params=PARAMS,
        name=name,
    )(*scalars, *arrays, *extra, *weights)


def regular(side, tokens, halos, perm, gains, weights):
    channels = tokens.shape[-1]
    half = perm.shape[0]
    keep = half - 72 if halos else half
    outs = [(2, keep, channels), (keep, channels), (keep, channels)]
    scratch = [
        pltpu.VMEM((2 * half, channels), BF),
        pltpu.VMEM((2 * half, 3 * channels), BF),
        pltpu.VMEM((2 * half, channels), BF),
        pltpu.VMEM((2, half, channels), F32),
    ]
    body = functools.partial(block0, keep)
    name = "regular_b" if halos else "regular_a"
    return call(body, name, [side], [tokens, *halos], [perm, gains], weights, 0, outs, scratch)


def room(count, channels):
    return [
        pltpu.VMEM((count * 144, channels), BF),
        pltpu.VMEM((count, 72, channels), F32),
        pltpu.VMEM((count * 144, 2 * channels), BF),
        pltpu.VMEM((count, 72, channels), F32),
    ]


def shifted_early(arrays, gains, weights):
    _, half, channels = arrays[0].shape
    count = 2 * (half // 72 - 1)
    outs = [(count * 72, channels)]
    return call(early, "early", [], arrays, [gains], weights, 1, outs, room(count, channels))[0]


def shifted_late(side, arrays, perm, gains, weights):
    _, kept, channels = arrays[2].shape
    count = 2 * (kept // 72 + 1)
    half = perm.shape[0]
    outs = [(2, 2, half // 2, channels)]
    scratch = room(count, channels) + [pltpu.VMEM((half, channels), F32)]
    return call(late, "late", [side], arrays, [perm, gains], weights, 1, outs, scratch)[0]


def shards(tokens, gains, w_qkv, w_proj, w_in, w_out):
    levels, height, breadth, channels = tokens.shape
    perm_a, perm_b, back = tables(breadth)
    weights = (w_qkv, w_proj, w_in, w_out)
    lats, lons = lax.axis_size("lat"), lax.axis_size("lon")
    place = lax.axis_index("lat")
    side = (place % 2).astype(jnp.int32).reshape(1)

    def column(part):
        part = part.reshape(levels, 2, SY, WX, channels).transpose(1, 0, 2, 3, 4)
        return part.reshape(2, 72, channels)

    def beside(part, distance):
        route = [((x + distance) % lons, x) for x in range(lons)]
        return lax.ppermute(column(part), "lon", route)

    def swap(block, first):
        route = []
        for y in range(first, lats - 1, 2):
            route += [(y, y + 1), (y + 1, y)]
        return lax.ppermute(block, "lat", route)

    left = beside(tokens[:, :, breadth - WX :], -1)
    right = beside(tokens[:, :, :WX], 1)
    tile = tokens.reshape(2, -1, channels)
    xa, ca, sa = regular(side, tile, [], perm_a, gains, weights)
    fca, fsa = swap(ca, 1), swap(sa, 0)
    xb, cb, sb = regular(side, tile, [right, left], perm_b, gains, weights)
    fcb, fsb = swap(cb, 1), swap(sb, 0)

    token = np.arange(72)
    lev = token % UNIT // (UNIT // 2)
    same = np.tile(lev[:, None] == lev[None, :], (1, 2))
    far = np.arange(144) >= 72
    step = 1 - 2 * (place % 2)
    partners = jnp.stack([place - step, place + step])
    dead = (partners < 0) | (partners >= lats)
    allowed = same[None] & ~(dead[:, None, None] & far[None, None, :])
    bias = jnp.where(allowed, 0.0, NEGATIVE).astype(F32)
    done = shifted_early([xa, ca, sa, fca, fsa, bias], gains, weights)
    out = shifted_late(
        side, [done, xa, xb, ca, sa, cb, sb, fca, fsa, fcb, fsb, bias], back, gains, weights
    )
    return out.reshape(tokens.shape)


def solution(mesh):
    in_specs = (P(None, "lat", "lon", None), P(), P(), P(), P(), P())
    out_specs = P(None, "lat", "lon", None)
    return jax.shard_map(shards, mesh=mesh, in_specs=in_specs, out_specs=out_specs, check_vma=False)
```

```python
import functools

import jax
import jax.numpy as jnp
import numpy as np
from jax import lax
from jax.experimental import pallas as pl
from jax.experimental.pallas import tpu as pltpu
from jax.sharding import PartitionSpec as P

HEADS = 16
WY = 12
WX = 6
SY = 6
SX = 3
EPSILON = 1e-05
LIMIT = 32 * 1024 * 1024
NEGATIVE = -1e30
BF = jnp.bfloat16
F32 = jnp.float32
UNIT = 36
WIDTH0 = 128
WIDTH1 = 256
EXP_SCALE = float(32.0 ** -0.5 * np.log2(np.e))


def norm(values, gain_row):
    centered = values - jnp.mean(values, axis=-1, keepdims=True)
    variance = jnp.mean(centered * centered, axis=-1, keepdims=True)
    return (centered * lax.rsqrt(variance + EPSILON) * gain_row).astype(BF)


def dot(a, b):
    return jnp.dot(a, b, preferred_element_type=F32)


def attend(q, k, v, bias, width):
    n, channels = q.shape
    head = channels // HEADS
    count = width // head
    lane = lax.broadcasted_iota(jnp.int32, (1, width), 1) // head
    lanes = lax.broadcasted_iota(jnp.int32, (n, width), 1) // head
    pieces = []
    for g in range(channels // width):
        cut = slice(width * g, width * (g + 1))
        qg = q[:, cut]
        stacked = jnp.concatenate(
            [qg * (lane == j).astype(F32) for j in range(count)], axis=0
        ).astype(BF)
        s = lax.dot_general(
            stacked, k[:, cut], (((1,), (1,)), ((), ())), preferred_element_type=F32
        )
        if bias is not None:
            s = s + jnp.concatenate([bias] * count, axis=0)
        p = jnp.exp2((s - jnp.max(s, axis=-1, keepdims=True)) * EXP_SCALE).astype(BF)
        vg = v[:, cut]
        o = dot(p, jnp.concatenate([vg, jnp.ones((vg.shape[0], 128), BF)], axis=1))
        scale = 1.0 / o[:, width:]
        if width > 128:
            scale = jnp.concatenate([scale] * (width // 128), axis=1)
        o = o[:, :width] * scale
        total = o[:n]
        for j in range(1, count):
            total = jnp.where(lanes == j, o[j * n : (j + 1) * n], total)
        pieces.append(total)
    return jnp.concatenate(pieces, axis=1)


def finish(x, attended, gain_row, w_proj, w_in, w_out):
    mixed = (x.astype(F32) + dot(attended, w_proj)).astype(BF)
    normed = norm(mixed.astype(F32), gain_row)
    h = dot(normed, w_in)
    h = jax.nn.gelu(h, approximate=True).astype(BF)
    return mixed.astype(F32) + dot(h, w_out)


def fetch(moves, sems):
    copies = [pltpu.make_async_copy(src, dst, sems.at[i]) for i, (src, dst) in enumerate(moves)]
    for copy in copies:
        copy.start()
    return copies


def weight_moves(refs, rooms, index):
    wqkv, *others = refs
    qkv_room, *other_rooms = rooms
    cut = qkv_room.shape[0] // 2
    parts = [slice(0, cut), slice(cut, 2 * cut)]
    return [(wqkv.at[index, p], qkv_room.at[p]) for p in parts] + [
        (w.at[index], room) for w, room in zip(others, other_rooms)
    ]


def block0(keep, side_ref, *refs):
    *halos, gains_ref, x_far, perm_far, wqkv_far, wproj_far, win_far, wout_far = refs[:-14]
    x1_ref, cross_ref, same_ref, xs, qkv, att, xf, x_ref, perm_ref = refs[-14:-5]
    wqkv_ref, wproj_ref, win_ref, wout_ref, sems = refs[-5:]
    moves = [(perm_far, perm_ref), (x_far.at[0], x_ref.at[0]), (x_far.at[1], x_ref.at[1])]
    rooms = (wqkv_ref, wproj_ref, win_ref, wout_ref)
    moves += weight_moves((wqkv_far, wproj_far, win_far, wout_far), rooms, 0)
    copies = fetch(moves, sems)
    tokens, channels = xs.shape
    half = tokens // 2
    strips = half // 72
    quarter = x_ref.shape[1] // 2
    for copy in copies[:3]:
        copy.wait()
    perm = perm_ref[...]
    parts = []
    for r in range(2):
        nat = [x_ref[z, quarter * r : quarter * (r + 1)] for z in range(2)]
        if halos:
            nat.append(
                jnp.concatenate([h[r].astype(F32) for h in halos], axis=0).astype(BF)
            )
        nat = jnp.concatenate(nat, axis=0)
        parts.append(dot(perm, nat).reshape(strips, 72, channels))
    x = jnp.concatenate(parts, axis=1).reshape(tokens, channels)
    xs[...] = x.astype(BF)
    normed = norm(x, gains_ref[0:1])
    for copy in copies[3:5]:
        copy.wait()
    qkv[...] = dot(normed, wqkv_ref[...]).astype(BF)

    def window(i, _):
        at = pl.ds(pl.multiple_of(i * 144, 16), 144)
        q = qkv[at, :channels].astype(F32)
        k, v = qkv[at, channels : 2 * channels], qkv[at, 2 * channels :]
        att[at] = attend(q, k, v, None, WIDTH0).astype(BF)
        return 0

    lax.fori_loop(0, strips, window, 0)
    for copy in copies[5:]:
        copy.wait()
    new = finish(xs[...], att[...], gains_ref[1:2], wproj_ref[...], win_ref[...], wout_ref[...])
    new = new.reshape(strips, 2, 72, channels)
    for r in range(2):
        xf[r] = new[:, r].reshape(half, channels)
    odd = side_ref[0]
    for g, n_ref in ((0, cross_ref), (1, same_ref)):
        mine = pltpu.roll(xf[jnp.where(odd == 0, g, 1 - g)], UNIT, 0).astype(BF)
        x1_ref[g] = mine[:keep]
        n_ref[...] = norm(mine.astype(F32), gains_ref[2:3])[:keep]


def blocks(rows):
    return rows.astype(F32).reshape(-1, 72, rows.shape[-1])


def windows(own, far, bias_ref, wqkv_ref, copies, lhs, qs, kv, os):
    count, _, channels = own.shape
    lhs[...] = jnp.concatenate([own, far], axis=1).reshape(count * 144, channels).astype(BF)
    for copy in copies:
        copy.wait()
    q = dot(own.reshape(count * 72, channels).astype(BF), wqkv_ref[:, :channels])
    qs[...] = q.astype(BF).astype(F32).reshape(count, 72, channels)
    rows = count * 72

    def project(i, _):
        at = pl.ds(pl.multiple_of(i * rows, 16), rows)
        kv[at] = dot(lhs[at], wqkv_ref[:, channels:]).astype(BF)
        return 0

    lax.fori_loop(0, 2, project, 0)

    def window(i, _):
        at = pl.ds(pl.multiple_of(i * 144, 16), 144)
        bias = bias_ref[i // (count // 2)]
        os[i] = attend(qs[i], kv[at, :channels], kv[at, channels:], bias, WIDTH1)
        return 0

    lax.fori_loop(0, count, window, 0)


def early(x_ref, cross_ref, same_ref, far_cross_ref, far_same_ref, bias_ref,
          gains_ref, wqkv_far, wproj_far, win_far, wout_far, out_ref, lhs, qs, kv, os,
          wqkv_ref, wproj_ref, win_ref, wout_ref, sems):
    channels = x_ref.shape[-1]
    rooms = (wqkv_ref, wproj_ref, win_ref, wout_ref)
    copies = fetch(weight_moves((wqkv_far, wproj_far, win_far, wout_far), rooms, 1), sems)

    def pair(a_ref, b_ref):
        return jnp.concatenate([blocks(a_ref[...])[1:], blocks(b_ref[...])[1:]], axis=0)

    own, far = pair(cross_ref, same_ref), pair(far_cross_ref, far_same_ref)
    windows(own, far, bias_ref, wqkv_ref, copies[:2], lhs, qs, kv, os)
    for copy in copies[2:]:
        copy.wait()
    rows = own.shape[0] * 72
    x = jnp.concatenate([blocks(x_ref[g])[1:] for g in range(2)], axis=0).reshape(rows, channels)
    attended = os[...].reshape(rows, channels).astype(BF)
    out_ref[...] = finish(
        x, attended, gains_ref[3:4], wproj_ref[...], win_ref[...], wout_ref[...]
    ).astype(BF)


def late(side_ref, done_ref, xa_ref, xb_ref, ca_ref, sa_ref, cb_ref, sb_ref,
         fca_ref, fsa_ref, fcb_ref, fsb_ref, bias_ref,
         gains_ref, perm_far, wqkv_far, wproj_far, win_far, wout_far,
         out_far, lhs, qs, kv, os, tile_ref, out_ref, perm_ref,
         wqkv_ref, wproj_ref, win_ref, wout_ref, sems):
    channels = xa_ref.shape[-1]
    rooms = (wqkv_ref, wproj_ref, win_ref, wout_ref)
    moves = weight_moves((wqkv_far, wproj_far, win_far, wout_far), rooms, 1)
    copies = fetch(moves + [(perm_far, perm_ref)], sems)
    first = lax.broadcasted_iota(jnp.int32, (72, channels), 0) < UNIT

    def extend(a, b):
        a, b = blocks(a), blocks(b)
        mid, lead = jnp.where(first, a[0], b[0]), jnp.where(first, b[0], a[0])
        return jnp.concatenate([mid[None], b[1:], lead[None]], axis=0)

    own = jnp.concatenate(
        [extend(ca_ref[...], cb_ref[...]), extend(sa_ref[...], sb_ref[...])], axis=0
    )
    far = jnp.concatenate(
        [extend(fca_ref[...], fcb_ref[...]), extend(fsa_ref[...], fsb_ref[...])], axis=0
    )
    windows(own, far, bias_ref, wqkv_ref, copies[:2], lhs, qs, kv, os)
    for copy in copies[2:]:
        copy.wait()
    count = own.shape[0] // 2
    last = count - 2
    xs, atts = [], []
    for g in range(2):
        a, b = blocks(xa_ref[g]), blocks(xb_ref[g])
        o = os[count * g : count * (g + 1)]
        xs += [
            jnp.where(first, b[last], a[0])[None],
            jnp.where(first, a[0], b[0])[None],
            b[1:last],
        ]
        atts += [jnp.where(first, o[last], o[count - 1])[None], o[:last]]
    rows = (count - 1) * 72
    x = jnp.concatenate(xs, axis=0).reshape(2 * rows, channels)
    attended = jnp.concatenate(atts, axis=0).reshape(2 * rows, channels).astype(BF)
    new = finish(x, attended, gains_ref[3:4], wproj_ref[...], win_ref[...], wout_ref[...])
    ready = done_ref[...].astype(F32)
    share = ready.shape[0] // 2
    odd = side_ref[0]
    sent = []
    for g in range(2):
        tile_ref[:72] = new[rows * g : rows * g + 72]
        tile_ref[72 : 72 + share] = ready[share * g : share * (g + 1)]
        tile_ref[72 + share :] = new[rows * g + 72 : rows * (g + 1)]
        nat = dot(perm_ref[...], tile_ref[...].astype(BF)).astype(BF)
        quarter = nat.shape[0] // 2
        r = jnp.where(odd == 0, g, 1 - g)
        for z in range(2):
            out_ref[g, z] = nat[quarter * z : quarter * (z + 1)]
            copy = pltpu.make_async_copy(out_ref.at[g, z], out_far.at[z, r], sems.at[2 * g + z])
            copy.start()
            sent.append(copy)
    for copy in sent:
        copy.wait()


def orders(strips):
    unit, lev, row, col = np.meshgrid(
        np.arange(2 * strips), np.arange(2), np.arange(SY), np.arange(SX), indexing="ij"
    )
    breadth = WX * strips
    return (lev * SY * breadth + row * breadth + unit * SX + col).reshape(-1)


def near(array):
    return pltpu.with_memory_space_constraint(array, pltpu.VMEM)


def tables(breadth):
    strips = breadth // WX
    order = orders(strips)
    half = order.size
    onehot = np.zeros((half, half), np.float32)
    onehot[np.arange(half), order] = 1.0
    cut = 72 * (strips // 2 + 1)
    halo = np.zeros((72, 72), np.float32)
    halo[np.arange(72), orders(1)] = 1.0
    rest = np.zeros((half - cut + 144, half + 144), np.float32)
    rest[: half - cut, :half] = onehot[cut:]
    rest[half - cut : half - cut + 72, half : half + 72] = halo
    rest[half - cut + 72 :, half + 72 :] = halo
    made = (onehot[:cut], rest, np.roll(onehot, UNIT, axis=0).T)
    return tuple(jnp.asarray(m, BF) for m in made)


PARAMS = pltpu.CompilerParams(vmem_limit_bytes=LIMIT)


def call(body, name, scalars, arrays, far, outs, scratch, keep=True):
    vmem, hbm = (pl.BlockSpec(memory_space=m) for m in (pltpu.VMEM, pltpu.HBM))
    weights = [pltpu.VMEM(w.shape[1:], BF) for w in far[-4:]]
    return pl.pallas_call(
        body,
        in_specs=[pl.BlockSpec(memory_space=pltpu.SMEM) for _ in scalars]
        + [vmem for _ in arrays]
        + [hbm for _ in far],
        out_specs=[vmem if keep else hbm for _ in outs],
        out_shape=[pltpu.VMEM(o, BF) if keep else pltpu.HBM(o, BF) for o in outs],
        scratch_shapes=scratch + weights + [pltpu.SemaphoreType.DMA((8,))],
        compiler_params=PARAMS,
        name=name,
    )(*scalars, *[near(a) for a in arrays], *[pltpu.with_memory_space_constraint(a, pltpu.HBM) for a in far])


def regular(side, tokens, halos, perm, gains, weights):
    channels = tokens.shape[-1]
    half = perm.shape[0]
    keep = half - 72 if halos else half
    outs = [(2, keep, channels), (keep, channels), (keep, channels)]
    scratch = [
        pltpu.VMEM((2 * half, channels), BF),
        pltpu.VMEM((2 * half, 3 * channels), BF),
        pltpu.VMEM((2 * half, channels), BF),
        pltpu.VMEM((2, half, channels), F32),
        pltpu.VMEM(tokens.shape, BF),
        pltpu.VMEM(perm.shape, BF),
    ]
    body = functools.partial(block0, keep)
    name = "regular_b" if halos else "regular_a"
    return call(
        body, name, [side], [*halos, gains], [tokens, perm, *weights], outs, scratch
    )


def room(count, channels):
    return [
        pltpu.VMEM((count * 144, channels), BF),
        pltpu.VMEM((count, 72, channels), F32),
        pltpu.VMEM((count * 144, 2 * channels), BF),
        pltpu.VMEM((count, 72, channels), F32),
    ]


def shifted_early(arrays, gains, weights):
    _, half, channels = arrays[0].shape
    count = 2 * (half // 72 - 1)
    outs = [(count * 72, channels)]
    return call(early, "early", [], [*arrays, gains], weights, outs, room(count, channels))[0]


def shifted_late(side, arrays, perm, gains, weights):
    _, kept, channels = arrays[2].shape
    count = 2 * (kept // 72 + 1)
    half = perm.shape[0]
    outs = [(2, 2, half // 2, channels)]
    scratch = room(count, channels) + [
        pltpu.VMEM((half, channels), F32),
        pltpu.VMEM(outs[0], BF),
        pltpu.VMEM(perm.shape, BF),
    ]
    far = [perm, *weights]
    return call(late, "late", [side], [*arrays, gains], far, outs, scratch, keep=False)[0]


def shards(tokens, gains, w_qkv, w_proj, w_in, w_out):
    levels, height, breadth, channels = tokens.shape
    perm_a, perm_b, back = tables(breadth)
    weights = [w_qkv, w_proj, w_in, w_out]
    lats, lons = lax.axis_size("lat"), lax.axis_size("lon")
    place = lax.axis_index("lat")
    side = (place % 2).astype(jnp.int32).reshape(1)

    def column(part):
        part = part.reshape(levels, 2, SY, WX, channels).transpose(1, 0, 2, 3, 4)
        return part.reshape(2, 72, channels)

    def beside(part, distance):
        route = [((x + distance) % lons, x) for x in range(lons)]
        return lax.ppermute(column(part), "lon", route)

    def swap(block, first):
        route = []
        for y in range(first, lats - 1, 2):
            route += [(y, y + 1), (y + 1, y)]
        return lax.ppermute(block, "lat", route)

    left = beside(tokens[:, :, breadth - WX :], -1)
    right = beside(tokens[:, :, :WX], 1)
    tile = tokens.reshape(2, -1, channels)
    xa, ca, sa = regular(side, tile, [], perm_a, gains, weights)
    fca, fsa = swap(ca, 1), swap(sa, 0)
    xb, cb, sb = regular(side, tile, [right, left], perm_b, gains, weights)
    fcb, fsb = swap(cb, 1), swap(sb, 0)

    token = np.arange(72)
    lev = token % UNIT // (UNIT // 2)
    same = np.tile(lev[:, None] == lev[None, :], (1, 2))
    far = np.arange(144) >= 72
    step = 1 - 2 * (place % 2)
    partners = jnp.stack([place - step, place + step])
    dead = (partners < 0) | (partners >= lats)
    allowed = same[None] & ~(dead[:, None, None] & far[None, None, :])
    bias = jnp.where(allowed, 0.0, NEGATIVE).astype(F32)
    done = shifted_early([xa, ca, sa, fca, fsa, bias], gains, weights)
    out = shifted_late(
        side, [done, xa, xb, ca, sa, cb, sb, fca, fsa, fcb, fsb, bias], back, gains, weights
    )
    return out.reshape(tokens.shape)


def solution(mesh):
    in_specs = (P(None, "lat", "lon", None), P(), P(), P(), P(), P())
    out_specs = P(None, "lat", "lon", None)
    return jax.shard_map(shards, mesh=mesh, in_specs=in_specs, out_specs=out_specs, check_vma=False)
```

```python
import functools

import jax
import jax.numpy as jnp
import numpy as np
from jax import lax
from jax.experimental import pallas as pl
from jax.experimental.pallas import tpu as pltpu
from jax.sharding import PartitionSpec as P

HEADS = 16
WY = 12
WX = 6
SY = 6
SX = 3
EPSILON = 1e-05
LIMIT = 32 * 1024 * 1024
NEGATIVE = -1e30
BF = jnp.bfloat16
F32 = jnp.float32
UNIT = 36
WIDTH0 = 128
WIDTH1 = 128
EXP_SCALE = float(32.0 ** -0.5 * np.log2(np.e))


def norm(values, gain_row):
    centered = values - jnp.mean(values, axis=-1, keepdims=True)
    variance = jnp.mean(centered * centered, axis=-1, keepdims=True)
    return (centered * lax.rsqrt(variance + EPSILON) * gain_row).astype(BF)


def dot(a, b):
    return jnp.dot(a, b, preferred_element_type=F32)


def attend(q, k, v, bias, width):
    n, channels = q.shape
    head = channels // HEADS
    count = width // head
    lane = lax.broadcasted_iota(jnp.int32, (1, width), 1) // head
    lanes = lax.broadcasted_iota(jnp.int32, (n, width), 1) // head
    pieces = []
    for g in range(channels // width):
        cut = slice(width * g, width * (g + 1))
        qg = q[:, cut]
        stacked = jnp.concatenate(
            [qg * (lane == j).astype(F32) for j in range(count)], axis=0
        ).astype(BF)
        s = lax.dot_general(
            stacked, k[:, cut], (((1,), (1,)), ((), ())), preferred_element_type=F32
        )
        if bias is not None:
            s = s + jnp.concatenate([bias] * count, axis=0)
        p = jnp.exp2((s - jnp.max(s, axis=-1, keepdims=True)) * EXP_SCALE).astype(BF)
        vg = v[:, cut]
        o = dot(p, jnp.concatenate([vg, jnp.ones((vg.shape[0], 128), BF)], axis=1))
        scale = 1.0 / o[:, width:]
        if width > 128:
            scale = jnp.concatenate([scale] * (width // 128), axis=1)
        o = o[:, :width] * scale
        total = o[:n]
        for j in range(1, count):
            total = jnp.where(lanes == j, o[j * n : (j + 1) * n], total)
        pieces.append(total)
    return jnp.concatenate(pieces, axis=1)


def finish(x, attended, gain_row, w_proj, w_in, w_out):
    mixed = (x.astype(F32) + dot(attended, w_proj)).astype(BF)
    normed = norm(mixed.astype(F32), gain_row)
    h = dot(normed, w_in)
    h = jax.nn.gelu(h, approximate=True).astype(BF)
    return mixed.astype(F32) + dot(h, w_out)


def fetch(moves, sems):
    copies = [pltpu.make_async_copy(src, dst, sems.at[i]) for i, (src, dst) in enumerate(moves)]
    for copy in copies:
        copy.start()
    return copies


def weight_moves(refs, rooms, index):
    wqkv, *others = refs
    qkv_room, *other_rooms = rooms
    cut = qkv_room.shape[0] // 2
    parts = [slice(0, cut), slice(cut, 2 * cut)]
    return [(wqkv.at[index, p], qkv_room.at[p]) for p in parts] + [
        (w.at[index], room) for w, room in zip(others, other_rooms)
    ]


def block0(keep, side_ref, *refs):
    *halos, gains_ref, x_far, perm_far, wqkv_far, wproj_far, win_far, wout_far = refs[:-14]
    x1_ref, cross_ref, same_ref, xs, qkv, att, xf, x_ref, perm_ref = refs[-14:-5]
    wqkv_ref, wproj_ref, win_ref, wout_ref, sems = refs[-5:]
    moves = [(perm_far, perm_ref), (x_far.at[0], x_ref.at[0]), (x_far.at[1], x_ref.at[1])]
    rooms = (wqkv_ref, wproj_ref, win_ref, wout_ref)
    moves += weight_moves((wqkv_far, wproj_far, win_far, wout_far), rooms, 0)
    copies = fetch(moves, sems)
    tokens, channels = xs.shape
    half = tokens // 2
    strips = half // 72
    quarter = x_ref.shape[1] // 2
    for copy in copies[:3]:
        copy.wait()
    perm = perm_ref[...]
    parts = []
    for r in range(2):
        nat = [x_ref[z, quarter * r : quarter * (r + 1)] for z in range(2)]
        if halos:
            nat.append(
                jnp.concatenate([h[r].astype(F32) for h in halos], axis=0).astype(BF)
            )
        nat = jnp.concatenate(nat, axis=0)
        parts.append(dot(perm, nat).reshape(strips, 72, channels))
    x = jnp.concatenate(parts, axis=1).reshape(tokens, channels)
    xs[...] = x.astype(BF)
    normed = norm(x, gains_ref[0:1])
    for copy in copies[3:5]:
        copy.wait()
    qkv[...] = dot(normed, wqkv_ref[...]).astype(BF)

    def window(i, _):
        at = pl.ds(pl.multiple_of(i * 144, 16), 144)
        q = qkv[at, :channels].astype(F32)
        k, v = qkv[at, channels : 2 * channels], qkv[at, 2 * channels :]
        att[at] = attend(q, k, v, None, WIDTH0).astype(BF)
        return 0

    lax.fori_loop(0, strips, window, 0, unroll=True)
    for copy in copies[5:]:
        copy.wait()
    new = finish(xs[...], att[...], gains_ref[1:2], wproj_ref[...], win_ref[...], wout_ref[...])
    new = new.reshape(strips, 2, 72, channels)
    for r in range(2):
        xf[r] = new[:, r].reshape(half, channels)
    odd = side_ref[0]
    for g, n_ref in ((0, cross_ref), (1, same_ref)):
        mine = pltpu.roll(xf[jnp.where(odd == 0, g, 1 - g)], UNIT, 0).astype(BF)
        x1_ref[g] = mine[:keep]
        n_ref[...] = norm(mine.astype(F32), gains_ref[2:3])[:keep]


def blocks(rows):
    return rows.astype(F32).reshape(-1, 72, rows.shape[-1])


def windows(own, far, bias_ref, wqkv_ref, copies, lhs, qs, kv, os):
    count, _, channels = own.shape
    lhs[...] = jnp.concatenate([own, far], axis=1).reshape(count * 144, channels).astype(BF)
    for copy in copies:
        copy.wait()
    q = dot(own.reshape(count * 72, channels).astype(BF), wqkv_ref[:, :channels])
    qs[...] = q.astype(BF).astype(F32).reshape(count, 72, channels)
    rows = count * 72

    def project(i, _):
        at = pl.ds(pl.multiple_of(i * rows, 16), rows)
        kv[at] = dot(lhs[at], wqkv_ref[:, channels:]).astype(BF)
        return 0

    lax.fori_loop(0, 2, project, 0, unroll=True)

    def window(i, _):
        at = pl.ds(pl.multiple_of(i * 144, 16), 144)
        bias = bias_ref[i // (count // 2)]
        os[i] = attend(qs[i], kv[at, :channels], kv[at, channels:], bias, WIDTH1)
        return 0

    lax.fori_loop(0, count, window, 0, unroll=True)


def early(x_ref, cross_ref, same_ref, far_cross_ref, far_same_ref, bias_ref,
          gains_ref, wqkv_far, wproj_far, win_far, wout_far, out_ref, lhs, qs, kv, os,
          wqkv_ref, wproj_ref, win_ref, wout_ref, sems):
    channels = x_ref.shape[-1]
    rooms = (wqkv_ref, wproj_ref, win_ref, wout_ref)
    copies = fetch(weight_moves((wqkv_far, wproj_far, win_far, wout_far), rooms, 1), sems)

    def pair(a_ref, b_ref):
        return jnp.concatenate([blocks(a_ref[...])[1:], blocks(b_ref[...])[1:]], axis=0)

    own, far = pair(cross_ref, same_ref), pair(far_cross_ref, far_same_ref)
    windows(own, far, bias_ref, wqkv_ref, copies[:2], lhs, qs, kv, os)
    for copy in copies[2:]:
        copy.wait()
    rows = own.shape[0] * 72
    x = jnp.concatenate([blocks(x_ref[g])[1:] for g in range(2)], axis=0).reshape(rows, channels)
    attended = os[...].reshape(rows, channels).astype(BF)
    out_ref[...] = finish(
        x, attended, gains_ref[3:4], wproj_ref[...], win_ref[...], wout_ref[...]
    ).astype(BF)


def late(side_ref, done_ref, xa_ref, xb_ref, ca_ref, sa_ref, cb_ref, sb_ref,
         fca_ref, fsa_ref, fcb_ref, fsb_ref, bias_ref,
         gains_ref, perm_far, wqkv_far, wproj_far, win_far, wout_far,
         out_far, lhs, qs, kv, os, tile_ref, out_ref, perm_ref,
         wqkv_ref, wproj_ref, win_ref, wout_ref, sems):
    channels = xa_ref.shape[-1]
    rooms = (wqkv_ref, wproj_ref, win_ref, wout_ref)
    moves = weight_moves((wqkv_far, wproj_far, win_far, wout_far), rooms, 1)
    copies = fetch(moves + [(perm_far, perm_ref)], sems)
    first = lax.broadcasted_iota(jnp.int32, (72, channels), 0) < UNIT

    def extend(a, b):
        a, b = blocks(a), blocks(b)
        mid, lead = jnp.where(first, a[0], b[0]), jnp.where(first, b[0], a[0])
        return jnp.concatenate([mid[None], b[1:], lead[None]], axis=0)

    own = jnp.concatenate(
        [extend(ca_ref[...], cb_ref[...]), extend(sa_ref[...], sb_ref[...])], axis=0
    )
    far = jnp.concatenate(
        [extend(fca_ref[...], fcb_ref[...]), extend(fsa_ref[...], fsb_ref[...])], axis=0
    )
    windows(own, far, bias_ref, wqkv_ref, copies[:2], lhs, qs, kv, os)
    for copy in copies[2:]:
        copy.wait()
    count = own.shape[0] // 2
    last = count - 2
    xs, atts = [], []
    for g in range(2):
        a, b = blocks(xa_ref[g]), blocks(xb_ref[g])
        o = os[count * g : count * (g + 1)]
        xs += [
            jnp.where(first, b[last], a[0])[None],
            jnp.where(first, a[0], b[0])[None],
            b[1:last],
        ]
        atts += [jnp.where(first, o[last], o[count - 1])[None], o[:last]]
    rows = (count - 1) * 72
    x = jnp.concatenate(xs, axis=0).reshape(2 * rows, channels)
    attended = jnp.concatenate(atts, axis=0).reshape(2 * rows, channels).astype(BF)
    new = finish(x, attended, gains_ref[3:4], wproj_ref[...], win_ref[...], wout_ref[...])
    ready = done_ref[...].astype(F32)
    share = ready.shape[0] // 2
    odd = side_ref[0]
    sent = []
    for g in range(2):
        tile_ref[:72] = new[rows * g : rows * g + 72]
        tile_ref[72 : 72 + share] = ready[share * g : share * (g + 1)]
        tile_ref[72 + share :] = new[rows * g + 72 : rows * (g + 1)]
        nat = dot(perm_ref[...], tile_ref[...].astype(BF)).astype(BF)
        quarter = nat.shape[0] // 2
        r = jnp.where(odd == 0, g, 1 - g)
        for z in range(2):
            out_ref[g, z] = nat[quarter * z : quarter * (z + 1)]
            copy = pltpu.make_async_copy(out_ref.at[g, z], out_far.at[z, r], sems.at[2 * g + z])
            copy.start()
            sent.append(copy)
    for copy in sent:
        copy.wait()


def orders(strips):
    unit, lev, row, col = np.meshgrid(
        np.arange(2 * strips), np.arange(2), np.arange(SY), np.arange(SX), indexing="ij"
    )
    breadth = WX * strips
    return (lev * SY * breadth + row * breadth + unit * SX + col).reshape(-1)


def near(array):
    return pltpu.with_memory_space_constraint(array, pltpu.VMEM)


def tables(breadth):
    strips = breadth // WX
    order = orders(strips)
    half = order.size
    onehot = np.zeros((half, half), np.float32)
    onehot[np.arange(half), order] = 1.0
    cut = 72 * (strips // 2 + 1)
    halo = np.zeros((72, 72), np.float32)
    halo[np.arange(72), orders(1)] = 1.0
    rest = np.zeros((half - cut + 144, half + 144), np.float32)
    rest[: half - cut, :half] = onehot[cut:]
    rest[half - cut : half - cut + 72, half : half + 72] = halo
    rest[half - cut + 72 :, half + 72 :] = halo
    made = (onehot[:cut], rest, np.roll(onehot, UNIT, axis=0).T)
    return tuple(jnp.asarray(m, BF) for m in made)


PARAMS = pltpu.CompilerParams(vmem_limit_bytes=LIMIT)


def call(body, name, scalars, arrays, far, outs, scratch, keep=True):
    vmem, hbm = (pl.BlockSpec(memory_space=m) for m in (pltpu.VMEM, pltpu.HBM))
    weights = [pltpu.VMEM(w.shape[1:], BF) for w in far[-4:]]
    return pl.pallas_call(
        body,
        in_specs=[pl.BlockSpec(memory_space=pltpu.SMEM) for _ in scalars]
        + [vmem for _ in arrays]
        + [hbm for _ in far],
        out_specs=[vmem if keep else hbm for _ in outs],
        out_shape=[pltpu.VMEM(o, BF) if keep else pltpu.HBM(o, BF) for o in outs],
        scratch_shapes=scratch + weights + [pltpu.SemaphoreType.DMA((8,))],
        compiler_params=PARAMS,
        name=name,
    )(*scalars, *[near(a) for a in arrays], *[pltpu.with_memory_space_constraint(a, pltpu.HBM) for a in far])


def regular(side, tokens, halos, perm, gains, weights):
    channels = tokens.shape[-1]
    half = perm.shape[0]
    keep = half - 72 if halos else half
    outs = [(2, keep, channels), (keep, channels), (keep, channels)]
    scratch = [
        pltpu.VMEM((2 * half, channels), BF),
        pltpu.VMEM((2 * half, 3 * channels), BF),
        pltpu.VMEM((2 * half, channels), BF),
        pltpu.VMEM((2, half, channels), F32),
        pltpu.VMEM(tokens.shape, BF),
        pltpu.VMEM(perm.shape, BF),
    ]
    body = functools.partial(block0, keep)
    name = "regular_b" if halos else "regular_a"
    return call(
        body, name, [side], [*halos, gains], [tokens, perm, *weights], outs, scratch
    )


def room(count, channels):
    return [
        pltpu.VMEM((count * 144, channels), BF),
        pltpu.VMEM((count, 72, channels), F32),
        pltpu.VMEM((count * 144, 2 * channels), BF),
        pltpu.VMEM((count, 72, channels), F32),
    ]


def shifted_early(arrays, gains, weights):
    _, half, channels = arrays[0].shape
    count = 2 * (half // 72 - 1)
    outs = [(count * 72, channels)]
    return call(early, "early", [], [*arrays, gains], weights, outs, room(count, channels))[0]


def shifted_late(side, arrays, perm, gains, weights):
    _, kept, channels = arrays[2].shape
    count = 2 * (kept // 72 + 1)
    half = perm.shape[0]
    outs = [(2, 2, half // 2, channels)]
    scratch = room(count, channels) + [
        pltpu.VMEM((half, channels), F32),
        pltpu.VMEM(outs[0], BF),
        pltpu.VMEM(perm.shape, BF),
    ]
    far = [perm, *weights]
    return call(late, "late", [side], [*arrays, gains], far, outs, scratch, keep=False)[0]


def shards(tokens, gains, w_qkv, w_proj, w_in, w_out):
    levels, height, breadth, channels = tokens.shape
    perm_a, perm_b, back = tables(breadth)
    weights = [w_qkv, w_proj, w_in, w_out]
    lats, lons = lax.axis_size("lat"), lax.axis_size("lon")
    place = lax.axis_index("lat")
    side = (place % 2).astype(jnp.int32).reshape(1)

    def column(part):
        part = part.reshape(levels, 2, SY, WX, channels).transpose(1, 0, 2, 3, 4)
        return part.reshape(2, 72, channels)

    def beside(part, distance):
        route = [((x + distance) % lons, x) for x in range(lons)]
        return lax.ppermute(column(part), "lon", route)

    def swap(block, first):
        route = []
        for y in range(first, lats - 1, 2):
            route += [(y, y + 1), (y + 1, y)]
        return lax.ppermute(block, "lat", route)

    left = beside(tokens[:, :, breadth - WX :], -1)
    right = beside(tokens[:, :, :WX], 1)
    tile = tokens.reshape(2, -1, channels)
    xa, ca, sa = regular(side, tile, [], perm_a, gains, weights)
    fca, fsa = swap(ca, 1), swap(sa, 0)
    xb, cb, sb = regular(side, tile, [right, left], perm_b, gains, weights)
    fcb, fsb = swap(cb, 1), swap(sb, 0)

    token = np.arange(72)
    lev = token % UNIT // (UNIT // 2)
    same = np.tile(lev[:, None] == lev[None, :], (1, 2))
    far = np.arange(144) >= 72
    step = 1 - 2 * (place % 2)
    partners = jnp.stack([place - step, place + step])
    dead = (partners < 0) | (partners >= lats)
    allowed = same[None] & ~(dead[:, None, None] & far[None, None, :])
    bias = jnp.where(allowed, 0.0, NEGATIVE).astype(F32)
    done = shifted_early([xa, ca, sa, fca, fsa, bias], gains, weights)
    out = shifted_late(
        side, [done, xa, xb, ca, sa, cb, sb, fca, fsa, fcb, fsb, bias], back, gains, weights
    )
    return out.reshape(tokens.shape)


def solution(mesh):
    in_specs = (P(None, "lat", "lon", None), P(), P(), P(), P(), P())
    out_specs = P(None, "lat", "lon", None)
    return jax.shard_map(shards, mesh=mesh, in_specs=in_specs, out_specs=out_specs, check_vma=False)
```

```python
import functools

import jax
import jax.numpy as jnp
import numpy as np
from jax import lax
from jax.experimental import pallas as pl
from jax.experimental.pallas import tpu as pltpu
from jax.sharding import PartitionSpec as P

HEADS = 16
WY = 12
WX = 6
SY = 6
SX = 3
EPSILON = 1e-05
LIMIT = 32 * 1024 * 1024
NEGATIVE = -1e30
BF = jnp.bfloat16
F32 = jnp.float32
UNIT = 36
WIDTH0 = 128
WIDTH1 = 128
EXP_SCALE = float(32.0 ** -0.5 * np.log2(np.e))


def norm(values, gain_row):
    centered = values - jnp.mean(values, axis=-1, keepdims=True)
    variance = jnp.mean(centered * centered, axis=-1, keepdims=True)
    return (centered * lax.rsqrt(variance + EPSILON) * gain_row).astype(BF)


def dot(a, b):
    return jnp.dot(a, b, preferred_element_type=F32)


def attend(q, k, v, bias, width):
    n, channels = q.shape
    head = channels // HEADS
    count = width // head
    lane = lax.broadcasted_iota(jnp.int32, (1, width), 1) // head
    lanes = lax.broadcasted_iota(jnp.int32, (n, width), 1) // head
    pieces = []
    for g in range(channels // width):
        cut = slice(width * g, width * (g + 1))
        qg = q[:, cut]
        stacked = jnp.concatenate(
            [qg * (lane == j).astype(F32) for j in range(count)], axis=0
        ).astype(BF)
        s = lax.dot_general(
            stacked, k[:, cut], (((1,), (1,)), ((), ())), preferred_element_type=F32
        )
        if bias is not None:
            s = s + jnp.concatenate([bias] * count, axis=0)
        p = jnp.exp2((s - jnp.max(s, axis=-1, keepdims=True)) * EXP_SCALE).astype(BF)
        vg = v[:, cut]
        o = dot(p, jnp.concatenate([vg, jnp.ones((vg.shape[0], 128), BF)], axis=1))
        scale = 1.0 / o[:, width:]
        if width > 128:
            scale = jnp.concatenate([scale] * (width // 128), axis=1)
        o = o[:, :width] * scale
        total = o[:n]
        for j in range(1, count):
            total = jnp.where(lanes == j, o[j * n : (j + 1) * n], total)
        pieces.append(total)
    return jnp.concatenate(pieces, axis=1)


def finish(x, attended, gain_row, w_proj, w_in, w_out):
    mixed = (x.astype(F32) + dot(attended, w_proj)).astype(BF)
    normed = norm(mixed.astype(F32), gain_row)
    h = dot(normed, w_in)
    h = jax.nn.gelu(h, approximate=True).astype(BF)
    return mixed.astype(F32) + dot(h, w_out)


def fetch(moves, sems):
    copies = [pltpu.make_async_copy(src, dst, sems.at[i]) for i, (src, dst) in enumerate(moves)]
    for copy in copies:
        copy.start()
    return copies


def weight_moves(refs, rooms, index):
    wqkv, *others = refs
    qkv_room, *other_rooms = rooms
    cut = qkv_room.shape[0] // 2
    parts = [slice(0, cut), slice(cut, 2 * cut)]
    return [(wqkv.at[index, p], qkv_room.at[p]) for p in parts] + [
        (w.at[index], room) for w, room in zip(others, other_rooms)
    ]


def block0(side_ref, *refs):
    gains_ref, x_far, perm_far, wqkv_far, wproj_far, win_far, wout_far = refs[:-14]
    x1_ref, cross_ref, same_ref, xs, qkv, att, xf, x_ref, perm_ref = refs[-14:-5]
    wqkv_ref, wproj_ref, win_ref, wout_ref, sems = refs[-5:]
    moves = [(perm_far, perm_ref), (x_far.at[0], x_ref.at[0]), (x_far.at[1], x_ref.at[1])]
    rooms = (wqkv_ref, wproj_ref, win_ref, wout_ref)
    moves += weight_moves((wqkv_far, wproj_far, win_far, wout_far), rooms, 0)
    copies = fetch(moves, sems)
    tokens, channels = xs.shape
    half = tokens // 2
    strips = half // 72
    quarter = x_ref.shape[1] // 2
    for copy in copies[:3]:
        copy.wait()
    perm = perm_ref[...]
    parts = []
    for r in range(2):
        nat = [x_ref[z, quarter * r : quarter * (r + 1)] for z in range(2)]
        nat = jnp.concatenate(nat, axis=0)
        parts.append(dot(perm, nat).reshape(strips, 72, channels))
    x = jnp.concatenate(parts, axis=1).reshape(tokens, channels)
    xs[...] = x.astype(BF)
    normed = norm(x, gains_ref[0:1])
    for copy in copies[3:5]:
        copy.wait()
    qkv[...] = dot(normed, wqkv_ref[...]).astype(BF)

    def window(i, _):
        at = pl.ds(pl.multiple_of(i * 144, 16), 144)
        q = qkv[at, :channels].astype(F32)
        k, v = qkv[at, channels : 2 * channels], qkv[at, 2 * channels :]
        att[at] = attend(q, k, v, None, WIDTH0).astype(BF)
        return 0

    lax.fori_loop(0, strips, window, 0, unroll=True)
    for copy in copies[5:]:
        copy.wait()
    new = finish(xs[...], att[...], gains_ref[1:2], wproj_ref[...], win_ref[...], wout_ref[...])
    new = new.reshape(strips, 2, 72, channels)
    for r in range(2):
        xf[r] = new[:, r].reshape(half, channels)
    odd = side_ref[0]
    for g, n_ref in ((0, cross_ref), (1, same_ref)):
        mine = pltpu.roll(xf[jnp.where(odd == 0, g, 1 - g)], UNIT, 0).astype(BF)
        x1_ref[g] = mine
        n_ref[...] = norm(mine.astype(F32), gains_ref[2:3])


def blocks(rows):
    return rows.astype(F32).reshape(-1, 72, rows.shape[-1])


def windows(own, far, bias_ref, wqkv_ref, copies, lhs, qs, kv, os):
    count, _, channels = own.shape
    lhs[...] = jnp.concatenate([own, far], axis=1).reshape(count * 144, channels).astype(BF)
    for copy in copies:
        copy.wait()
    q = dot(own.reshape(count * 72, channels).astype(BF), wqkv_ref[:, :channels])
    qs[...] = q.astype(BF).astype(F32).reshape(count, 72, channels)
    rows = count * 72

    def project(i, _):
        at = pl.ds(pl.multiple_of(i * rows, 16), rows)
        kv[at] = dot(lhs[at], wqkv_ref[:, channels:]).astype(BF)
        return 0

    lax.fori_loop(0, 2, project, 0, unroll=True)

    def window(i, _):
        at = pl.ds(pl.multiple_of(i * 144, 16), 144)
        bias = bias_ref[i // (count // 2)]
        os[i] = attend(qs[i], kv[at, :channels], kv[at, channels:], bias, WIDTH1)
        return 0

    lax.fori_loop(0, count, window, 0, unroll=True)


def early(x_ref, cross_ref, same_ref, far_cross_ref, far_same_ref, bias_ref,
          gains_ref, wqkv_far, wproj_far, win_far, wout_far, out_ref, lhs, qs, kv, os,
          wqkv_ref, wproj_ref, win_ref, wout_ref, sems):
    channels = x_ref.shape[-1]
    rooms = (wqkv_ref, wproj_ref, win_ref, wout_ref)
    copies = fetch(weight_moves((wqkv_far, wproj_far, win_far, wout_far), rooms, 1), sems)

    def inner(rows):
        part = blocks(rows)
        return [part[1:2], part[3:4]]

    def pair(a_ref, b_ref):
        return jnp.concatenate(inner(a_ref[...]) + inner(b_ref[...]), axis=0)

    own, far = pair(cross_ref, same_ref), pair(far_cross_ref, far_same_ref)
    windows(own, far, bias_ref, wqkv_ref, copies[:2], lhs, qs, kv, os)
    for copy in copies[2:]:
        copy.wait()
    rows = own.shape[0] * 72
    x = jnp.concatenate(inner(x_ref[0]) + inner(x_ref[1]), axis=0).reshape(rows, channels)
    attended = os[...].reshape(rows, channels).astype(BF)
    out_ref[...] = finish(
        x, attended, gains_ref[3:4], wproj_ref[...], win_ref[...], wout_ref[...]
    ).astype(BF)


def late(side_ref, done_ref, xa_ref, xb_ref, ca_ref, sa_ref, cb_ref, sb_ref,
         fca_ref, fsa_ref, fcb_ref, fsb_ref, left_ref, right_ref, bias_ref,
         gains_ref, perm_far, wqkv_far, wproj_far, win_far, wout_far,
         out_far, lhs, qs, kv, os, tile_ref, out_ref, perm_ref,
         wqkv_ref, wproj_ref, win_ref, wout_ref, sems):
    channels = xa_ref.shape[-1]
    rooms = (wqkv_ref, wproj_ref, win_ref, wout_ref)
    moves = weight_moves((wqkv_far, wproj_far, win_far, wout_far), rooms, 1)
    copies = fetch(moves + [(perm_far, perm_ref)], sems)
    first = lax.broadcasted_iota(jnp.int32, (72, channels), 0) < UNIT

    def inside(a, b):
        near_side = jnp.where(first, a[0], b[0])
        far_side = jnp.where(first, b[0], a[0])
        return [near_side[None], b[1:], far_side[None]]

    def extend(a_ref, b_ref, index):
        a, b = blocks(a_ref[...]), blocks(b_ref[...])
        lead = jnp.where(first, left_ref[index].astype(F32), a[2])
        tail = jnp.where(first, a[2], right_ref[index].astype(F32))
        return inside(a, b) + [lead[None], tail[None]]

    own = jnp.concatenate(extend(ca_ref, cb_ref, 0) + extend(sa_ref, sb_ref, 1), axis=0)
    far = jnp.concatenate(extend(fca_ref, fcb_ref, 2) + extend(fsa_ref, fsb_ref, 3), axis=0)
    windows(own, far, bias_ref, wqkv_ref, copies[:2], lhs, qs, kv, os)
    for copy in copies[2:]:
        copy.wait()
    count = own.shape[0] // 2
    last = count - 2
    xs, atts = [], []
    for g in range(2):
        a, b = blocks(xa_ref[g]), blocks(xb_ref[g])
        o = os[count * g : count * (g + 1)]
        xs += [a[2:3]] + inside(a, b)
        atts += [jnp.where(first, o[last + 1], o[last])[None], o[:last]]
    rows = (count - 1) * 72
    x = jnp.concatenate(xs, axis=0).reshape(2 * rows, channels)
    attended = jnp.concatenate(atts, axis=0).reshape(2 * rows, channels).astype(BF)
    new = finish(x, attended, gains_ref[3:4], wproj_ref[...], win_ref[...], wout_ref[...])
    ready = done_ref[...].astype(F32)
    odd = side_ref[0]
    sent = []
    for g in range(2):
        tile_ref[:72] = new[rows * g : rows * g + 72]
        tile_ref[72:144] = ready[144 * g + 72 : 144 * (g + 1)]
        tile_ref[144 : 72 + rows] = new[rows * g + 72 : rows * (g + 1)]
        tile_ref[72 + rows :] = ready[144 * g : 144 * g + 72]
        nat = dot(perm_ref[...], tile_ref[...].astype(BF)).astype(BF)
        quarter = nat.shape[0] // 2
        r = jnp.where(odd == 0, g, 1 - g)
        for z in range(2):
            out_ref[g, z] = nat[quarter * z : quarter * (z + 1)]
            copy = pltpu.make_async_copy(out_ref.at[g, z], out_far.at[z, r], sems.at[2 * g + z])
            copy.start()
            sent.append(copy)
    for copy in sent:
        copy.wait()


def orders(strips):
    unit, lev, row, col = np.meshgrid(
        np.arange(2 * strips), np.arange(2), np.arange(SY), np.arange(SX), indexing="ij"
    )
    breadth = WX * strips
    return (lev * SY * breadth + row * breadth + unit * SX + col).reshape(-1)


def near(array):
    return pltpu.with_memory_space_constraint(array, pltpu.VMEM)


def tables(breadth):
    strips = breadth // WX
    order = orders(strips)
    half = order.size
    onehot = np.zeros((half, half), np.float32)
    onehot[np.arange(half), order] = 1.0
    outer = np.concatenate([onehot[half - 144 :], onehot[:144]])
    made = (outer, onehot[144 : half - 144], np.roll(onehot, UNIT, axis=0).T)
    return tuple(jnp.asarray(m, BF) for m in made)


PARAMS = pltpu.CompilerParams(vmem_limit_bytes=LIMIT)


def call(body, name, scalars, arrays, far, outs, scratch, keep=True):
    vmem, hbm = (pl.BlockSpec(memory_space=m) for m in (pltpu.VMEM, pltpu.HBM))
    weights = [pltpu.VMEM(w.shape[1:], BF) for w in far[-4:]]
    return pl.pallas_call(
        body,
        in_specs=[pl.BlockSpec(memory_space=pltpu.SMEM) for _ in scalars]
        + [vmem for _ in arrays]
        + [hbm for _ in far],
        out_specs=[vmem if keep else hbm for _ in outs],
        out_shape=[pltpu.VMEM(o, BF) if keep else pltpu.HBM(o, BF) for o in outs],
        scratch_shapes=scratch + weights + [pltpu.SemaphoreType.DMA((8,))],
        compiler_params=PARAMS,
        name=name,
    )(*scalars, *[near(a) for a in arrays], *[pltpu.with_memory_space_constraint(a, pltpu.HBM) for a in far])


def regular(name, side, tokens, perm, gains, weights):
    channels = tokens.shape[-1]
    half = perm.shape[0]
    outs = [(2, half, channels), (half, channels), (half, channels)]
    scratch = [
        pltpu.VMEM((2 * half, channels), BF),
        pltpu.VMEM((2 * half, 3 * channels), BF),
        pltpu.VMEM((2 * half, channels), BF),
        pltpu.VMEM((2, half, channels), F32),
        pltpu.VMEM(tokens.shape, BF),
        pltpu.VMEM(perm.shape, BF),
    ]
    return call(block0, name, [side], [gains], [tokens, perm, *weights], outs, scratch)


def room(count, channels):
    return [
        pltpu.VMEM((count * 144, channels), BF),
        pltpu.VMEM((count, 72, channels), F32),
        pltpu.VMEM((count * 144, 2 * channels), BF),
        pltpu.VMEM((count, 72, channels), F32),
    ]


def shifted_early(arrays, gains, weights):
    channels = arrays[0].shape[-1]
    count = 4
    outs = [(count * 72, channels)]
    return call(early, "early", [], [*arrays, gains], weights, outs, room(count, channels))[0]


def shifted_late(side, arrays, perm, gains, weights):
    _, kept, channels = arrays[2].shape
    count = 2 * (kept // 72 + 3)
    half = perm.shape[0]
    outs = [(2, 2, half // 2, channels)]
    scratch = room(count, channels) + [
        pltpu.VMEM((half, channels), F32),
        pltpu.VMEM(outs[0], BF),
        pltpu.VMEM(perm.shape, BF),
    ]
    far = [perm, *weights]
    return call(late, "late", [side], [*arrays, gains], far, outs, scratch, keep=False)[0]


def shards(tokens, gains, w_qkv, w_proj, w_in, w_out):
    breadth, channels = tokens.shape[2:]
    outer, inner, back = tables(breadth)
    weights = [w_qkv, w_proj, w_in, w_out]
    lats, lons = lax.axis_size("lat"), lax.axis_size("lon")
    place = lax.axis_index("lat")
    side = (place % 2).astype(jnp.int32).reshape(1)

    def beside(part, distance):
        route = [((x + distance) % lons, x) for x in range(lons)]
        return lax.ppermute(part, "lon", route)

    def swap(block, first):
        route = []
        for y in range(first, lats - 1, 2):
            route += [(y, y + 1), (y + 1, y)]
        return lax.ppermute(block, "lat", route)

    tile = tokens.reshape(2, -1, channels)
    xa, ca, sa = regular("outer", side, tile, outer, gains, weights)
    fca, fsa = swap(ca, 1), swap(sa, 0)
    xb, cb, sb = regular("inner", side, tile, inner, gains, weights)
    fcb, fsb = swap(cb, 1), swap(sb, 0)
    edge = jnp.stack([part[144:216] for part in (ca, sa, fca, fsa)])
    left, right = beside(edge, -1), beside(edge, 1)

    token = np.arange(72)
    lev = token % UNIT // (UNIT // 2)
    same = np.tile(lev[:, None] == lev[None, :], (1, 2))
    far = np.arange(144) >= 72
    step = 1 - 2 * (place % 2)
    partners = jnp.stack([place - step, place + step])
    dead = (partners < 0) | (partners >= lats)
    allowed = same[None] & ~(dead[:, None, None] & far[None, None, :])
    bias = jnp.where(allowed, 0.0, NEGATIVE).astype(F32)
    done = shifted_early([xa, ca, sa, fca, fsa, bias], gains, weights)
    arrays = [done, xa, xb, ca, sa, cb, sb, fca, fsa, fcb, fsb, left, right, bias]
    out = shifted_late(side, arrays, back, gains, weights)
    return out.reshape(tokens.shape)


def solution(mesh):
    in_specs = (P(None, "lat", "lon", None), P(), P(), P(), P(), P())
    out_specs = P(None, "lat", "lon", None)
    return jax.shard_map(shards, mesh=mesh, in_specs=in_specs, out_specs=out_specs, check_vma=False)
```

```python
import functools

import jax
import jax.numpy as jnp
import numpy as np
from jax import lax
from jax.experimental import pallas as pl
from jax.experimental.pallas import tpu as pltpu
from jax.sharding import PartitionSpec as P

HEADS = 16
WY = 12
WX = 6
SY = 6
SX = 3
EPSILON = 1e-05
LIMIT = 32 * 1024 * 1024
NEGATIVE = -1e30
BF = jnp.bfloat16
F32 = jnp.float32
UNIT = 36
WIDTH0 = 128
WIDTH1 = 128
EXP_SCALE = float(32.0 ** -0.5 * np.log2(np.e))


def norm(values, gain_row):
    centered = values - jnp.mean(values, axis=-1, keepdims=True)
    variance = jnp.mean(centered * centered, axis=-1, keepdims=True)
    return (centered * lax.rsqrt(variance + EPSILON) * gain_row).astype(BF)


def dot(a, b):
    return jnp.dot(a, b, preferred_element_type=F32)


def attend(q, k, v, bias, width):
    n, channels = q.shape
    head = channels // HEADS
    count = width // head
    lane = lax.broadcasted_iota(jnp.int32, (1, width), 1) // head
    lanes = lax.broadcasted_iota(jnp.int32, (n, width), 1) // head
    pieces = []
    for g in range(channels // width):
        cut = slice(width * g, width * (g + 1))
        qg = q[:, cut]
        stacked = jnp.concatenate(
            [qg * (lane == j).astype(F32) for j in range(count)], axis=0
        ).astype(BF)
        s = lax.dot_general(
            stacked, k[:, cut], (((1,), (1,)), ((), ())), preferred_element_type=F32
        )
        if bias is not None:
            s = s + jnp.concatenate([bias] * count, axis=0)
        p = jnp.exp2((s - jnp.max(s, axis=-1, keepdims=True)) * EXP_SCALE).astype(BF)
        vg = v[:, cut]
        o = dot(p, jnp.concatenate([vg, jnp.ones((vg.shape[0], 128), BF)], axis=1))
        scale = 1.0 / o[:, width:]
        if width > 128:
            scale = jnp.concatenate([scale] * (width // 128), axis=1)
        o = o[:, :width] * scale
        total = o[:n]
        for j in range(1, count):
            total = jnp.where(lanes == j, o[j * n : (j + 1) * n], total)
        pieces.append(total)
    return jnp.concatenate(pieces, axis=1)


def finish(x, attended, gain_row, w_proj, w_in, w_out):
    mixed = (x.astype(F32) + dot(attended, w_proj)).astype(BF)
    normed = norm(mixed.astype(F32), gain_row)
    h = dot(normed, w_in)
    h = jax.nn.gelu(h, approximate=True).astype(BF)
    return mixed.astype(F32) + dot(h, w_out)


def fetch(moves, sems):
    copies = [pltpu.make_async_copy(src, dst, sems.at[i]) for i, (src, dst) in enumerate(moves)]
    for copy in copies:
        copy.start()
    return copies


def weight_moves(refs, rooms, index):
    wqkv, *others = refs
    qkv_room, *other_rooms = rooms
    cut = qkv_room.shape[0] // 2
    parts = [slice(0, cut), slice(cut, 2 * cut)]
    return [(wqkv.at[index, p], qkv_room.at[p]) for p in parts] + [
        (w.at[index], room) for w, room in zip(others, other_rooms)
    ]


def block0(side_ref, *refs):
    gains_far, x_far, perm_far, wqkv_far, wproj_far, win_far, wout_far = refs[:-15]
    x1_ref, cross_ref, same_ref, xs, qkv, att, xf, x_ref, perm_ref = refs[-15:-6]
    gains_ref, wqkv_ref, wproj_ref, win_ref, wout_ref, sems = refs[-6:]
    moves = [(gains_far, gains_ref), (perm_far, perm_ref)]
    moves += [(x_far.at[z], x_ref.at[z]) for z in range(2)]
    rooms = (wqkv_ref, wproj_ref, win_ref, wout_ref)
    moves += weight_moves((wqkv_far, wproj_far, win_far, wout_far), rooms, 0)
    copies = fetch(moves, sems)
    tokens, channels = xs.shape
    half = tokens // 2
    strips = half // 72
    quarter = x_ref.shape[1] // 2
    for copy in copies[:4]:
        copy.wait()
    perm = perm_ref[...]
    parts = []
    for r in range(2):
        nat = [x_ref[z, quarter * r : quarter * (r + 1)] for z in range(2)]
        nat = jnp.concatenate(nat, axis=0)
        parts.append(dot(perm, nat).reshape(strips, 72, channels))
    x = jnp.concatenate(parts, axis=1).reshape(tokens, channels)
    xs[...] = x.astype(BF)
    normed = norm(x, gains_ref[0:1])
    for copy in copies[4:6]:
        copy.wait()
    qkv[...] = dot(normed, wqkv_ref[...]).astype(BF)

    def window(i, _):
        at = pl.ds(pl.multiple_of(i * 144, 16), 144)
        q = qkv[at, :channels].astype(F32)
        k, v = qkv[at, channels : 2 * channels], qkv[at, 2 * channels :]
        att[at] = attend(q, k, v, None, WIDTH0).astype(BF)
        return 0

    lax.fori_loop(0, strips, window, 0, unroll=True)
    for copy in copies[6:]:
        copy.wait()
    new = finish(xs[...], att[...], gains_ref[1:2], wproj_ref[...], win_ref[...], wout_ref[...])
    new = new.reshape(strips, 2, 72, channels)
    for r in range(2):
        xf[r] = new[:, r].reshape(half, channels)
    odd = side_ref[0]
    for g, n_ref in ((0, cross_ref), (1, same_ref)):
        mine = pltpu.roll(xf[jnp.where(odd == 0, g, 1 - g)], UNIT, 0).astype(BF)
        x1_ref[g] = mine
        n_ref[...] = norm(mine.astype(F32), gains_ref[2:3])


def blocks(rows):
    return rows.astype(F32).reshape(-1, 72, rows.shape[-1])


def windows(own, far, bias_ref, wqkv_ref, copies, lhs, qs, kv, os):
    count, _, channels = own.shape
    lhs[...] = jnp.concatenate([own, far], axis=1).reshape(count * 144, channels).astype(BF)
    for copy in copies:
        copy.wait()
    q = dot(own.reshape(count * 72, channels).astype(BF), wqkv_ref[:, :channels])
    qs[...] = q.astype(BF).astype(F32).reshape(count, 72, channels)
    rows = count * 72

    def project(i, _):
        at = pl.ds(pl.multiple_of(i * rows, 16), rows)
        kv[at] = dot(lhs[at], wqkv_ref[:, channels:]).astype(BF)
        return 0

    lax.fori_loop(0, 2, project, 0, unroll=True)

    def window(i, _):
        at = pl.ds(pl.multiple_of(i * 144, 16), 144)
        bias = bias_ref[i // (count // 2)]
        os[i] = attend(qs[i], kv[at, :channels], kv[at, channels:], bias, WIDTH1)
        return 0

    lax.fori_loop(0, count, window, 0, unroll=True)


def early(x_ref, cross_ref, same_ref, far_cross_ref, far_same_ref, bias_ref,
          gains_ref, wqkv_far, wproj_far, win_far, wout_far, out_ref, lhs, qs, kv, os,
          wqkv_ref, wproj_ref, win_ref, wout_ref, sems):
    channels = x_ref.shape[-1]
    rooms = (wqkv_ref, wproj_ref, win_ref, wout_ref)
    moves = weight_moves((wqkv_far, wproj_far, win_far, wout_far), rooms, 1)
    copies = fetch(moves, sems)

    def inner(rows):
        part = blocks(rows)
        return [part[1:2], part[3:4]]

    def pair(a_ref, b_ref):
        return jnp.concatenate(inner(a_ref[...]) + inner(b_ref[...]), axis=0)

    own, far = pair(cross_ref, same_ref), pair(far_cross_ref, far_same_ref)
    windows(own, far, bias_ref, wqkv_ref, copies[:2], lhs, qs, kv, os)
    for copy in copies[2:]:
        copy.wait()
    rows = own.shape[0] * 72
    x = jnp.concatenate(inner(x_ref[0]) + inner(x_ref[1]), axis=0).reshape(rows, channels)
    attended = os[...].reshape(rows, channels).astype(BF)
    out_ref[...] = finish(
        x, attended, gains_ref[3:4], wproj_ref[...], win_ref[...], wout_ref[...]
    ).astype(BF)


def late(side_ref, done_ref, xa_ref, xb_ref, ca_ref, sa_ref, cb_ref, sb_ref,
         fca_ref, fsa_ref, fcb_ref, fsb_ref, left_ref, right_ref, bias_ref,
         gains_ref, perm_far, wqkv_far, wproj_far, win_far, wout_far,
         out_far, lhs, qs, kv, os, tile_ref, out_ref, perm_ref,
         wqkv_ref, wproj_ref, win_ref, wout_ref, sems):
    channels = xa_ref.shape[-1]
    rooms = (wqkv_ref, wproj_ref, win_ref, wout_ref)
    moves = weight_moves((wqkv_far, wproj_far, win_far, wout_far), rooms, 1)
    copies = fetch(moves + [(perm_far, perm_ref)], sems)
    first = lax.broadcasted_iota(jnp.int32, (72, channels), 0) < UNIT

    def inside(a, b):
        near_side = jnp.where(first, a[0], b[0])
        far_side = jnp.where(first, b[0], a[0])
        return [near_side[None], b[1:], far_side[None]]

    def extend(a_ref, b_ref, index):
        a, b = blocks(a_ref[...]), blocks(b_ref[...])
        lead = jnp.where(first, left_ref[index].astype(F32), a[2])
        tail = jnp.where(first, a[2], right_ref[index].astype(F32))
        return inside(a, b) + [lead[None], tail[None]]

    own = jnp.concatenate(extend(ca_ref, cb_ref, 0) + extend(sa_ref, sb_ref, 1), axis=0)
    far = jnp.concatenate(extend(fca_ref, fcb_ref, 2) + extend(fsa_ref, fsb_ref, 3), axis=0)
    windows(own, far, bias_ref, wqkv_ref, copies[:2], lhs, qs, kv, os)
    for copy in copies[2:]:
        copy.wait()
    count = own.shape[0] // 2
    last = count - 2
    xs, atts = [], []
    for g in range(2):
        a, b = blocks(xa_ref[g]), blocks(xb_ref[g])
        o = os[count * g : count * (g + 1)]
        xs += [a[2:3]] + inside(a, b)
        atts += [jnp.where(first, o[last + 1], o[last])[None], o[:last]]
    rows = (count - 1) * 72
    x = jnp.concatenate(xs, axis=0).reshape(2 * rows, channels)
    attended = jnp.concatenate(atts, axis=0).reshape(2 * rows, channels).astype(BF)
    new = finish(x, attended, gains_ref[3:4], wproj_ref[...], win_ref[...], wout_ref[...])
    ready = done_ref[...].astype(F32)
    odd = side_ref[0]
    sent = []
    for g in range(2):
        tile_ref[:72] = new[rows * g : rows * g + 72]
        tile_ref[72:144] = ready[144 * g + 72 : 144 * (g + 1)]
        tile_ref[144 : 72 + rows] = new[rows * g + 72 : rows * (g + 1)]
        tile_ref[72 + rows :] = ready[144 * g : 144 * g + 72]
        nat = dot(perm_ref[...], tile_ref[...].astype(BF)).astype(BF)
        quarter = nat.shape[0] // 2
        r = jnp.where(odd == 0, g, 1 - g)
        for z in range(2):
            out_ref[g, z] = nat[quarter * z : quarter * (z + 1)]
            copy = pltpu.make_async_copy(out_ref.at[g, z], out_far.at[z, r], sems.at[2 * g + z])
            copy.start()
            sent.append(copy)
    for copy in sent:
        copy.wait()


def orders(strips):
    unit, lev, row, col = np.meshgrid(
        np.arange(2 * strips), np.arange(2), np.arange(SY), np.arange(SX), indexing="ij"
    )
    breadth = WX * strips
    return (lev * SY * breadth + row * breadth + unit * SX + col).reshape(-1)


def near(array):
    return pltpu.with_memory_space_constraint(array, pltpu.VMEM)


def tables(breadth):
    strips = breadth // WX
    order = orders(strips)
    half = order.size
    onehot = np.zeros((half, half), np.float32)
    onehot[np.arange(half), order] = 1.0
    outer = np.concatenate([onehot[half - 144 :], onehot[:144]])
    made = (outer, onehot[144 : half - 144], np.roll(onehot, UNIT, axis=0).T)
    return tuple(jnp.asarray(m, BF) for m in made)


PARAMS = pltpu.CompilerParams(vmem_limit_bytes=LIMIT)


def call(body, name, scalars, arrays, far, weights, outs, scratch, keep=True):
    far = [*far, *weights]
    vmem, hbm = (pl.BlockSpec(memory_space=m) for m in (pltpu.VMEM, pltpu.HBM))
    space = pltpu.VMEM if keep else pltpu.HBM
    kept = [pltpu.VMEM(w.shape[1:], BF) for w in weights]
    return pl.pallas_call(
        body,
        in_specs=[pl.BlockSpec(memory_space=pltpu.SMEM) for _ in scalars]
        + [vmem for _ in arrays]
        + [hbm for _ in far],
        out_specs=[vmem if keep else hbm for _ in outs],
        out_shape=[space(*o) for o in outs],
        scratch_shapes=scratch + kept + [pltpu.SemaphoreType.DMA((10,))],
        compiler_params=PARAMS,
        name=name,
    )(
        *scalars,
        *[near(a) for a in arrays],
        *[pltpu.with_memory_space_constraint(a, pltpu.HBM) for a in far],
    )


def regular(name, scalars, tokens, perm, gains, weights):
    channels = tokens.shape[-1]
    half = perm.shape[0]
    shapes = [(2, half, channels), (half, channels), (half, channels)]
    outs = [(shape, BF) for shape in shapes]
    scratch = [
        pltpu.VMEM((2 * half, channels), BF),
        pltpu.VMEM((2 * half, 3 * channels), BF),
        pltpu.VMEM((2 * half, channels), BF),
        pltpu.VMEM((2, half, channels), F32),
        pltpu.VMEM(tokens.shape, BF),
        pltpu.VMEM(perm.shape, BF),
        pltpu.VMEM(gains.shape, F32),
    ]
    return call(block0, name, scalars, [], [gains, tokens, perm], weights, outs, scratch)


def room(count, channels):
    return [
        pltpu.VMEM((count * 144, channels), BF),
        pltpu.VMEM((count, 72, channels), F32),
        pltpu.VMEM((count * 144, 2 * channels), BF),
        pltpu.VMEM((count, 72, channels), F32),
    ]


def shifted_early(arrays, gains, weights):
    channels = arrays[0].shape[-1]
    count = 4
    outs = [((count * 72, channels), BF)]
    return call(early, "early", [], [*arrays, gains], [], weights, outs, room(count, channels))[0]


def shifted_late(side, arrays, perm, gains, weights):
    _, kept, channels = arrays[2].shape
    count = 2 * (kept // 72 + 3)
    half = perm.shape[0]
    shape = (2, 2, half // 2, channels)
    scratch = room(count, channels) + [
        pltpu.VMEM((half, channels), F32),
        pltpu.VMEM(shape, BF),
        pltpu.VMEM(perm.shape, BF),
    ]
    arrays, outs = [*arrays, gains], [(shape, BF)]
    return call(late, "late", [side], arrays, [perm], weights, outs, scratch, keep=False)[0]


def shards(tokens, gains, w_qkv, w_proj, w_in, w_out):
    breadth, channels = tokens.shape[2:]
    outer, inner, back = tables(breadth)
    weights = [w_qkv, w_proj, w_in, w_out]
    lats, lons = lax.axis_size("lat"), lax.axis_size("lon")
    place = lax.axis_index("lat")
    side = (place % 2).astype(jnp.int32).reshape(1)

    def beside(part, distance):
        route = [((x + distance) % lons, x) for x in range(lons)]
        return lax.ppermute(part, "lon", route)

    def swap(block, first):
        route = []
        for y in range(first, lats - 1, 2):
            route += [(y, y + 1), (y + 1, y)]
        return lax.ppermute(block, "lat", route)

    step = 1 - 2 * (place % 2)
    partners = jnp.stack([place - step, place + step])
    dead = (partners < 0) | (partners >= lats)
    token = np.arange(72)
    lev = token % UNIT // (UNIT // 2)
    same = np.tile(lev[:, None] == lev[None, :], (1, 2))
    live = np.stack([same, same & (np.arange(144) < 72)])
    table = jnp.asarray(np.where(live, 0.0, NEGATIVE), F32)
    bias = jnp.where(dead[:, None, None], table[1], table[0])

    tile = tokens.reshape(2, -1, channels)
    xa, ca, sa = regular("outer", [side], tile, outer, gains, weights)
    fca, fsa = swap(ca, 1), swap(sa, 0)
    xb, cb, sb = regular("inner", [side], tile, inner, gains, weights)
    sb, bias = lax.optimization_barrier((sb, bias))
    fcb, fsb = swap(cb, 1), swap(sb, 0)
    edge = jnp.stack([part[144:216] for part in (ca, sa, fca, fsa)])
    left, right = beside(edge, -1), beside(edge, 1)

    done = shifted_early([xa, ca, sa, fca, fsa, bias], gains, weights)
    arrays = [done, xa, xb, ca, sa, cb, sb, fca, fsa, fcb, fsb, left, right, bias]
    out = shifted_late(side, arrays, back, gains, weights)
    return out.reshape(tokens.shape)


def solution(mesh):
    in_specs = (P(None, "lat", "lon", None), P(), P(), P(), P(), P())
    out_specs = P(None, "lat", "lon", None)
    return jax.shard_map(shards, mesh=mesh, in_specs=in_specs, out_specs=out_specs, check_vma=False)
```

```python
import functools

import jax
import jax.numpy as jnp
import numpy as np
from jax import lax
from jax.experimental import pallas as pl
from jax.experimental.pallas import tpu as pltpu
from jax.sharding import PartitionSpec as P

HEADS = 16
WY = 12
WX = 6
SY = 6
SX = 3
EPSILON = 1e-05
LIMIT = 32 * 1024 * 1024
NEGATIVE = -1e30
BF = jnp.bfloat16
F32 = jnp.float32
UNIT = 36
WIDTH0 = 128
WIDTH1 = 128
EXP_SCALE = float(32.0 ** -0.5 * np.log2(np.e))


def norm(values, gain_row):
    centered = values - jnp.mean(values, axis=-1, keepdims=True)
    variance = jnp.mean(centered * centered, axis=-1, keepdims=True)
    return (centered * lax.rsqrt(variance + EPSILON) * gain_row).astype(BF)


def dot(a, b):
    return jnp.dot(a, b, preferred_element_type=F32)


def attend(q, k, v, bias, width):
    n, channels = q.shape
    head = channels // HEADS
    count = width // head
    lane = lax.broadcasted_iota(jnp.int32, (1, width), 1) // head
    lanes = lax.broadcasted_iota(jnp.int32, (n, width), 1) // head
    pieces = []
    for g in range(channels // width):
        cut = slice(width * g, width * (g + 1))
        qg = q[:, cut]
        stacked = jnp.concatenate(
            [qg * (lane == j).astype(F32) for j in range(count)], axis=0
        ).astype(BF)
        s = lax.dot_general(
            stacked, k[:, cut], (((1,), (1,)), ((), ())), preferred_element_type=F32
        )
        if bias is not None:
            s = s + jnp.concatenate([bias] * count, axis=0)
        p = jnp.exp2((s - jnp.max(s, axis=-1, keepdims=True)) * EXP_SCALE).astype(BF)
        vg = v[:, cut]
        o = dot(p, jnp.concatenate([vg, jnp.ones((vg.shape[0], 128), BF)], axis=1))
        scale = 1.0 / o[:, width:]
        if width > 128:
            scale = jnp.concatenate([scale] * (width // 128), axis=1)
        o = o[:, :width] * scale
        total = o[:n]
        for j in range(1, count):
            total = jnp.where(lanes == j, o[j * n : (j + 1) * n], total)
        pieces.append(total)
    return jnp.concatenate(pieces, axis=1)


def finish(x, attended, gain_row, w_proj, w_in, w_out):
    mixed = (x.astype(F32) + dot(attended, w_proj)).astype(BF)
    normed = norm(mixed.astype(F32), gain_row)
    h = dot(normed, w_in)
    h = jax.nn.gelu(h, approximate=True).astype(BF)
    return mixed.astype(F32) + dot(h, w_out)


def fetch(moves, sems):
    copies = [pltpu.make_async_copy(src, dst, sems.at[i]) for i, (src, dst) in enumerate(moves)]
    for copy in copies:
        copy.start()
    return copies


def weight_moves(refs, rooms, index):
    wqkv, *others = refs
    qkv_room, *other_rooms = rooms
    cut = qkv_room.shape[0] // 2
    parts = [slice(0, cut), slice(cut, 2 * cut)]
    return [(wqkv.at[index, p], qkv_room.at[p]) for p in parts] + [
        (w.at[index], room) for w, room in zip(others, other_rooms)
    ]


def block0(side_ref, *refs):
    gains_far, x_far, perm_far, wqkv_far, wproj_far, win_far, wout_far = refs[:-15]
    x1_ref, cross_ref, same_ref, xs, qkv, att, xf, x_ref, perm_ref = refs[-15:-6]
    gains_ref, wqkv_ref, wproj_ref, win_ref, wout_ref, sems = refs[-6:]
    moves = [(gains_far, gains_ref), (perm_far, perm_ref)]
    moves += [(x_far.at[z], x_ref.at[z]) for z in range(2)]
    rooms = (wqkv_ref, wproj_ref, win_ref, wout_ref)
    moves += weight_moves((wqkv_far, wproj_far, win_far, wout_far), rooms, 0)
    copies = fetch(moves, sems)
    tokens, channels = xs.shape
    half = tokens // 2
    strips = half // 72
    quarter = x_ref.shape[1] // 2
    for copy in copies[:4]:
        copy.wait()
    perm = perm_ref[...]
    parts = []
    for r in range(2):
        nat = [x_ref[z, quarter * r : quarter * (r + 1)] for z in range(2)]
        nat = jnp.concatenate(nat, axis=0)
        parts.append(dot(perm, nat).reshape(strips, 72, channels))
    x = jnp.concatenate(parts, axis=1).reshape(tokens, channels)
    xs[...] = x.astype(BF)
    normed = norm(x, gains_ref[0:1])
    for copy in copies[4:6]:
        copy.wait()
    qkv[...] = dot(normed, wqkv_ref[...]).astype(BF)

    def window(i, _):
        at = pl.ds(pl.multiple_of(i * 144, 16), 144)
        q = qkv[at, :channels].astype(F32)
        k, v = qkv[at, channels : 2 * channels], qkv[at, 2 * channels :]
        att[at] = attend(q, k, v, None, WIDTH0).astype(BF)
        return 0

    lax.fori_loop(0, strips, window, 0, unroll=True)
    for copy in copies[6:]:
        copy.wait()
    new = finish(xs[...], att[...], gains_ref[1:2], wproj_ref[...], win_ref[...], wout_ref[...])
    new = new.reshape(strips, 2, 72, channels)
    for r in range(2):
        xf[r] = new[:, r].reshape(half, channels)
    odd = side_ref[0]
    for g, n_ref in ((0, cross_ref), (1, same_ref)):
        mine = pltpu.roll(xf[jnp.where(odd == 0, g, 1 - g)], UNIT, 0).astype(BF)
        x1_ref[g] = mine
        n_ref[...] = norm(mine.astype(F32), gains_ref[2:3])


def blocks(rows):
    return rows.astype(F32).reshape(-1, 72, rows.shape[-1])


def windows(own, far, bias_ref, wqkv_ref, copies, lhs, qs, kv, os):
    count, _, channels = own.shape
    lhs[...] = jnp.concatenate([own, far], axis=1).reshape(count * 144, channels).astype(BF)
    for copy in copies:
        copy.wait()
    q = dot(own.reshape(count * 72, channels).astype(BF), wqkv_ref[:, :channels])
    qs[...] = q.astype(BF).astype(F32).reshape(count, 72, channels)
    rows = count * 72

    def project(i, _):
        at = pl.ds(pl.multiple_of(i * rows, 16), rows)
        kv[at] = dot(lhs[at], wqkv_ref[:, channels:]).astype(BF)
        return 0

    lax.fori_loop(0, 2, project, 0, unroll=True)

    def window(i, _):
        at = pl.ds(pl.multiple_of(i * 144, 16), 144)
        bias = bias_ref[i // (count // 2)]
        os[i] = attend(qs[i], kv[at, :channels], kv[at, channels:], bias, WIDTH1)
        return 0

    lax.fori_loop(0, count, window, 0, unroll=True)


def early(x_ref, cross_ref, same_ref, far_cross_ref, far_same_ref, bias_ref,
          gains_ref, wqkv_far, wproj_far, win_far, wout_far, out_ref, lhs, qs, kv, os,
          wqkv_ref, wproj_ref, win_ref, wout_ref, sems):
    channels = x_ref.shape[-1]
    rooms = (wqkv_ref, wproj_ref, win_ref, wout_ref)
    moves = weight_moves((wqkv_far, wproj_far, win_far, wout_far), rooms, 1)
    copies = fetch(moves, sems)

    def inner(rows):
        part = blocks(rows)
        return [part[1:2], part[3:4]]

    def pair(a_ref, b_ref):
        return jnp.concatenate(inner(a_ref[...]) + inner(b_ref[...]), axis=0)

    own, far = pair(cross_ref, same_ref), pair(far_cross_ref, far_same_ref)
    windows(own, far, bias_ref, wqkv_ref, copies[:2], lhs, qs, kv, os)
    for copy in copies[2:]:
        copy.wait()
    rows = own.shape[0] * 72
    x = jnp.concatenate(inner(x_ref[0]) + inner(x_ref[1]), axis=0).reshape(rows, channels)
    attended = os[...].reshape(rows, channels).astype(BF)
    out_ref[...] = finish(
        x, attended, gains_ref[3:4], wproj_ref[...], win_ref[...], wout_ref[...]
    ).astype(BF)


def late(side_ref, done_ref, xa_ref, xb_ref, ca_ref, sa_ref, cb_ref, sb_ref,
         fca_ref, fsa_ref, fcb_ref, fsb_ref, left_ref, right_ref, bias_ref,
         gains_ref, wqkv_ref, perm_far, wproj_far, win_far, wout_far,
         out_far, lhs, qs, kv, os, tile_ref, out_ref, perm_ref,
         wproj_ref, win_ref, wout_ref, sems):
    channels = xa_ref.shape[-1]
    pairs = ((wproj_far, wproj_ref), (win_far, win_ref), (wout_far, wout_ref))
    moves = [(w.at[1], room) for w, room in pairs]
    copies = fetch(moves + [(perm_far, perm_ref)], sems)
    first = lax.broadcasted_iota(jnp.int32, (72, channels), 0) < UNIT

    def inside(a, b):
        near_side = jnp.where(first, a[0], b[0])
        far_side = jnp.where(first, b[0], a[0])
        return [near_side[None], b[1:], far_side[None]]

    def extend(a_ref, b_ref, index):
        a, b = blocks(a_ref[...]), blocks(b_ref[...])
        lead = jnp.where(first, left_ref[index].astype(F32), a[2])
        tail = jnp.where(first, a[2], right_ref[index].astype(F32))
        return inside(a, b) + [lead[None], tail[None]]

    own = jnp.concatenate(extend(ca_ref, cb_ref, 0) + extend(sa_ref, sb_ref, 1), axis=0)
    far = jnp.concatenate(extend(fca_ref, fcb_ref, 2) + extend(fsa_ref, fsb_ref, 3), axis=0)
    windows(own, far, bias_ref, wqkv_ref.at[1], [], lhs, qs, kv, os)
    for copy in copies:
        copy.wait()
    count = own.shape[0] // 2
    last = count - 2
    xs, atts = [], []
    for g in range(2):
        a, b = blocks(xa_ref[g]), blocks(xb_ref[g])
        o = os[count * g : count * (g + 1)]
        xs += [a[2:3]] + inside(a, b)
        atts += [jnp.where(first, o[last + 1], o[last])[None], o[:last]]
    rows = (count - 1) * 72
    x = jnp.concatenate(xs, axis=0).reshape(2 * rows, channels)
    attended = jnp.concatenate(atts, axis=0).reshape(2 * rows, channels).astype(BF)
    new = finish(x, attended, gains_ref[3:4], wproj_ref[...], win_ref[...], wout_ref[...])
    ready = done_ref[...].astype(F32)
    odd = side_ref[0]
    sent = []
    for g in range(2):
        tile_ref[:72] = new[rows * g : rows * g + 72]
        tile_ref[72:144] = ready[144 * g + 72 : 144 * (g + 1)]
        tile_ref[144 : 72 + rows] = new[rows * g + 72 : rows * (g + 1)]
        tile_ref[72 + rows :] = ready[144 * g : 144 * g + 72]
        nat = dot(perm_ref[...], tile_ref[...].astype(BF)).astype(BF)
        quarter = nat.shape[0] // 2
        r = jnp.where(odd == 0, g, 1 - g)
        for z in range(2):
            out_ref[g, z] = nat[quarter * z : quarter * (z + 1)]
            copy = pltpu.make_async_copy(out_ref.at[g, z], out_far.at[z, r], sems.at[2 * g + z])
            copy.start()
            sent.append(copy)
    for copy in sent:
        copy.wait()


def orders(strips):
    unit, lev, row, col = np.meshgrid(
        np.arange(2 * strips), np.arange(2), np.arange(SY), np.arange(SX), indexing="ij"
    )
    breadth = WX * strips
    return (lev * SY * breadth + row * breadth + unit * SX + col).reshape(-1)


def near(array):
    return pltpu.with_memory_space_constraint(array, pltpu.VMEM)


def tables(breadth):
    strips = breadth // WX
    order = orders(strips)
    half = order.size
    onehot = np.zeros((half, half), np.float32)
    onehot[np.arange(half), order] = 1.0
    outer = np.concatenate([onehot[half - 144 :], onehot[:144]])
    made = (outer, onehot[144 : half - 144], np.roll(onehot, UNIT, axis=0).T)
    return tuple(jnp.asarray(m, BF) for m in made)


PARAMS = pltpu.CompilerParams(vmem_limit_bytes=LIMIT)


def call(body, name, scalars, arrays, far, weights, outs, scratch, keep=True):
    far = [*far, *weights]
    vmem, hbm = (pl.BlockSpec(memory_space=m) for m in (pltpu.VMEM, pltpu.HBM))
    space = pltpu.VMEM if keep else pltpu.HBM
    kept = [pltpu.VMEM(w.shape[1:], BF) for w in weights]
    return pl.pallas_call(
        body,
        in_specs=[pl.BlockSpec(memory_space=pltpu.SMEM) for _ in scalars]
        + [vmem for _ in arrays]
        + [hbm for _ in far],
        out_specs=[vmem if keep else hbm for _ in outs],
        out_shape=[space(*o) for o in outs],
        scratch_shapes=scratch + kept + [pltpu.SemaphoreType.DMA((10,))],
        compiler_params=PARAMS,
        name=name,
    )(
        *scalars,
        *[near(a) for a in arrays],
        *[pltpu.with_memory_space_constraint(a, pltpu.HBM) for a in far],
    )


def regular(name, scalars, tokens, perm, gains, weights):
    channels = tokens.shape[-1]
    half = perm.shape[0]
    shapes = [(2, half, channels), (half, channels), (half, channels)]
    outs = [(shape, BF) for shape in shapes]
    scratch = [
        pltpu.VMEM((2 * half, channels), BF),
        pltpu.VMEM((2 * half, 3 * channels), BF),
        pltpu.VMEM((2 * half, channels), BF),
        pltpu.VMEM((2, half, channels), F32),
        pltpu.VMEM(tokens.shape, BF),
        pltpu.VMEM(perm.shape, BF),
        pltpu.VMEM(gains.shape, F32),
    ]
    return call(block0, name, scalars, [], [gains, tokens, perm], weights, outs, scratch)


def room(count, channels):
    return [
        pltpu.VMEM((count * 144, channels), BF),
        pltpu.VMEM((count, 72, channels), F32),
        pltpu.VMEM((count * 144, 2 * channels), BF),
        pltpu.VMEM((count, 72, channels), F32),
    ]


def shifted_early(arrays, gains, weights):
    channels = arrays[0].shape[-1]
    count = 4
    outs = [((count * 72, channels), BF)]
    return call(early, "early", [], [*arrays, gains], [], weights, outs, room(count, channels))[0]


def shifted_late(side, arrays, perm, gains, weights):
    _, kept, channels = arrays[2].shape
    count = 2 * (kept // 72 + 3)
    half = perm.shape[0]
    shape = (2, 2, half // 2, channels)
    scratch = room(count, channels) + [
        pltpu.VMEM((half, channels), F32),
        pltpu.VMEM(shape, BF),
        pltpu.VMEM(perm.shape, BF),
    ]
    arrays, outs = [*arrays, gains, weights[0]], [(shape, BF)]
    return call(late, "late", [side], arrays, [perm], weights[1:], outs, scratch, keep=False)[0]


def shards(tokens, gains, w_qkv, w_proj, w_in, w_out):
    breadth, channels = tokens.shape[2:]
    outer, inner, back = tables(breadth)
    weights = [w_qkv, w_proj, w_in, w_out]
    lats, lons = lax.axis_size("lat"), lax.axis_size("lon")
    place = lax.axis_index("lat")
    side = (place % 2).astype(jnp.int32).reshape(1)

    def beside(part, distance):
        route = [((x + distance) % lons, x) for x in range(lons)]
        return lax.ppermute(part, "lon", route)

    def swap(block, first):
        route = []
        for y in range(first, lats - 1, 2):
            route += [(y, y + 1), (y + 1, y)]
        return lax.ppermute(block, "lat", route)

    step = 1 - 2 * (place % 2)
    partners = jnp.stack([place - step, place + step])
    dead = (partners < 0) | (partners >= lats)
    token = np.arange(72)
    lev = token % UNIT // (UNIT // 2)
    same = np.tile(lev[:, None] == lev[None, :], (1, 2))
    live = np.stack([same, same & (np.arange(144) < 72)])
    table = jnp.asarray(np.where(live, 0.0, NEGATIVE), F32)
    bias = jnp.where(dead[:, None, None], table[1], table[0])

    tile = tokens.reshape(2, -1, channels)
    xa, ca, sa = regular("outer", [side], tile, outer, gains, weights)
    fca, fsa = swap(ca, 1), swap(sa, 0)
    xb, cb, sb = regular("inner", [side], tile, inner, gains, weights)
    sb, bias = lax.optimization_barrier((sb, bias))
    fcb, fsb = swap(cb, 1), swap(sb, 0)
    edge = jnp.stack([part[144:216] for part in (ca, sa, fca, fsa)])
    left, right = beside(edge, -1), beside(edge, 1)

    done = shifted_early([xa, ca, sa, fca, fsa, bias], gains, weights)
    arrays = [done, xa, xb, ca, sa, cb, sb, fca, fsa, fcb, fsb, left, right, bias]
    out = shifted_late(side, arrays, back, gains, weights)
    return out.reshape(tokens.shape)


def solution(mesh):
    in_specs = (P(None, "lat", "lon", None), P(), P(), P(), P(), P())
    out_specs = P(None, "lat", "lon", None)
    return jax.shard_map(shards, mesh=mesh, in_specs=in_specs, out_specs=out_specs, check_vma=False)
```
